32 devices in a mesh: dp: 8 (over y, x, core), fsdp: 4 (over z).
Axes of the slice: x: 2, y: 2, z: 4, core: 2. Of those that a mesh axis runs over, the one named last changes fastest.
Arguments:
- waveform: bfloat16 [1024, 50], P(('dp', 'fsdp')), may hold values from -6 to 6
- destination: int32 [1024, 1], P(('dp', 'fsdp')), may hold values from 0 to 7; in each aligned block of 32 rows (0 to 31, 32 to 63, ...) at most 8 rows name the same one
- lengths: int32 [1024], P(('dp', 'fsdp')), may hold values from 20 to 50
- conv0_weight: bfloat16 [10, 512], replicated, may hold values from -2 to 2
- conv1_weight: bfloat16 [1536, 512], replicated, may hold values from -0.15625 to 0.15625
- norm_gain: float32 [3, 512], replicated, may hold values from 0.1 to 1.9
- norm_bias: float32 [3, 512], replicated, may hold values from -3 to 3
- proj_weight: bfloat16 [512, 1920], P(None, 'fsdp'), may hold values from -0.25 to 0.25
- proj_bias: bfloat16 [1920], P('fsdp'), may hold values from -3 to 3
- cotangent: bfloat16 [2048, 4, 1920], P(('dp', 'fsdp')), may hold values from -0.1875 to 0.1875
Outputs:
- features: bfloat16 [2048, 4, 1920], P(('dp', 'fsdp'))
- grad_proj_weight: bfloat16 [512, 1920], P(None, 'fsdp')
- grad_proj_bias: bfloat16 [1920], P('fsdp')
The draws below stay inside these ranges and needn't reach their ends.
Inputs may be any that keep to these rules, and one draw needn't show every extreme that they name: On each device no destination is named by more than 8 of its rows, and on some devices one destination is named by exactly 8 rows.
All inputs are finite; a program needn't handle non-finite values.
Results may differ from the reference program's by a relative error of at most 0.0064.
Values may be sent and summed in bfloat16 or wider, within the bound.
A program may use at most 64 MiB of HBM per device.

```python
import math
import jax
import jax.numpy as jnp
import numpy as np
from jax import lax

D_CONV = 512
D_MODEL = 1920
FR = 4
ROWS_DEV = 32
CAP = 8
SAMP = 50
ROWS = 1024
SLOTS = 2048
N_DP = 8
N_FSDP = 4


def with_ends(drawn, own_key, smallest, high):
    dims = drawn.shape
    index_at = [jax.random.randint(jax.random.fold_in(own_key, axis), (), 0, dims[axis]) for axis in range(len(dims))]
    drawn = drawn.at[tuple(index_at)].set(smallest)
    longest = dims.index(max(dims))
    index_at[longest] = (index_at[longest] + 1) % dims[longest]
    return drawn.at[tuple(index_at)].set(high)


def strengthened(drawn, own_key, source, target, blocks, factor):
    owner, partner = [(jnp.arange(drawn.shape[dim]) // (drawn.shape[dim] // blocks)).reshape([-1 if axis == dim else 1 for axis in range(drawn.ndim)]) for dim in (source, target)]
    chosen = jax.random.permutation(own_key, blocks)[partner]
    strong = (owner == chosen) | (owner == (partner + blocks // 2) % blocks)
    return jnp.where(strong, factor * drawn, drawn)


def level_of(key, shape, pieces, low, largest):
    def one(axis_at, parts):
        draws = jax.random.uniform(jax.random.fold_in(jax.random.fold_in(key, 6), axis_at), (parts,), jnp.float32, low / len(pieces), largest / len(pieces))
        return jnp.repeat(jnp.exp(draws), shape[axis_at] // parts).reshape((-1,) + (1,) * (len(shape) - axis_at - 1))

    loudness = one(*pieces[0])
    for cut in pieces[1:]:
        loudness = loudness * one(*cut)
    return loudness


def routed_block(key, own, number, rows, number_of, top, most, skew):
    sequence = jax.random.permutation(key, number_of)
    heavy_load, usual = shares(number_of, rows * top, most, skew, True), shares(number_of, rows * top, most, skew, False)
    places = jnp.arange(number_of)

    def named(sizes, offset_by):
        used = int((sizes > 0).sum())
        fixed = max(1, used // 4)
        moved = fixed + (places - fixed + offset_by * (used - fixed)) % max(1, number_of - fixed)
        return jnp.zeros((number_of,), jnp.int32).at[sequence[jnp.where(places < fixed, places, moved)]].set(jnp.asarray(sizes, jnp.int32))

    sizes = jnp.where(number % 4 == 0, named(heavy_load, number // 4), named(usual, number - number // 4 - 1))
    mixed = jax.random.permutation(jax.random.fold_in(own, 3), number_of)
    donor, sink = mixed[0:number_of // 2 * 2:2], mixed[1:number_of // 2 * 2:2]
    margin = jnp.minimum(sizes[donor] - 1, most - sizes[sink]) // 2
    margin = jnp.where((donor == sequence[0]) | (sink == sequence[0]) | (sizes[sink] == 0), 0, jnp.maximum(margin, 0))
    moved = jax.random.randint(jax.random.fold_in(own, 4), (number_of // 2,), 0, 1 << 20) % (margin + 1)
    sizes = sizes.at[donor].add(-moved).at[sink].add(moved)
    members = jnp.searchsorted(jnp.cumsum(sizes), jnp.arange(rows * top), side="right").astype(jnp.int32)
    listing = members.reshape(top, rows).T
    listing = listing[jax.random.permutation(jax.random.fold_in(own, 1), rows)]
    offset_by = jax.random.randint(jax.random.fold_in(own, 2), (rows, 1), 0, top)
    return jnp.take_along_axis(listing, (jnp.arange(top)[None, :] + offset_by) % top, axis=1)


def shares(amount, total, reach, lean, full):
    weights = [(1 << 20) // math.isqrt(standing ** lean) + 1 for standing in range(1, amount + 1)]
    largest = reach if full else min(reach, max(-(-total // amount), total * weights[0] // sum(weights)))
    least = 1 if total - largest >= amount - 1 else 0
    counts, spare = [largest] + [least] * (amount - 1), total - largest - least * (amount - 1)
    while spare > 0:
        candidates = [i for i in range(1, amount) if counts[i] < largest] or [i for i in range(1, amount) if counts[i] < reach]
        whole, left = sum([weights[i] for i in candidates]), spare
        for i in candidates:
            more = min(reach - counts[i], max(1, left * weights[i] // whole), spare)
            counts[i] = counts[i] + more
            spare = spare - more
    return np.array(counts)


def scatter_about(own_key, dims, spread, bound, cuts=(), held_as=jnp.bfloat16):
    array = spread * jax.random.normal(own_key, dims, jnp.float32)
    if cuts:
        array = array * level_of(own_key, dims, cuts, -0.22, 0.18)
    return jnp.clip(array, -bound, bound).astype(held_as)


def gaussian_with(rng, shape, scale, limit, cuts, heavy, kind=jnp.bfloat16):
    result = scale * jax.random.normal(rng, shape, jnp.float32)
    if cuts:
        result = result * level_of(rng, shape, cuts, -0.22, 0.18)
    return jnp.clip(strengthened(result, jax.random.fold_in(rng, 3), *heavy), -limit, limit).astype(kind)


def setup_inputs(seed: int = 0) -> dict:
    seeds = jax.random.split(jax.random.key(seed), 11)
    waveform = scatter_about(seeds[0], (ROWS, SAMP), 1.0, 6.0, ((0, 32),))
    destination_keys = jax.random.split(jax.random.fold_in(seeds[1], 1), ROWS // ROWS_DEV)
    destination_turns = jax.random.permutation(jax.random.fold_in(seeds[1], 3), ROWS // ROWS_DEV)
    destination = jax.vmap(lambda own, number: routed_block(jax.random.fold_in(seeds[1], 2), own, number, ROWS_DEV, N_DP, 1, CAP, 2))(destination_keys, destination_turns).reshape((ROWS, 1))
    lengths = with_ends(jax.random.randint(seeds[2], (ROWS,), 20, SAMP + 1), jax.random.fold_in(seeds[2], 1), 20, SAMP).astype(jnp.int32)
    conv0_weight = scatter_about(seeds[3], (10, D_CONV), 10 ** -0.5, 2.0)
    conv1_weight = scatter_about(seeds[4], (3 * D_CONV, D_CONV), (3 * D_CONV) ** -0.5, 0.15625)
    norm_gain = jnp.clip(1.0 + 0.18 * jax.random.normal(seeds[5], (3, D_CONV), jnp.float32), 0.1, 1.9)
    norm_bias = scatter_about(seeds[6], (3, D_CONV), 0.5, 3.0, (), jnp.float32)
    proj_weight = scatter_about(seeds[7], (D_CONV, D_MODEL), D_CONV ** -0.5, 0.25, ((1, 4),))
    proj_bias = scatter_about(seeds[8], (D_MODEL,), 0.5, 3.0, ((0, 4),))
    cotangent = gaussian_with(seeds[9], (SLOTS, FR, D_MODEL), (ROWS * FR) ** -0.5, 0.1875, ((0, 32),), (0, 2, 32, 2.75))
    return dict(waveform=waveform, destination=destination, lengths=lengths, conv0_weight=conv0_weight, conv1_weight=conv1_weight, norm_gain=norm_gain, norm_bias=norm_bias, proj_weight=proj_weight, proj_bias=proj_bias, cotangent=cotangent)


def layer_norm(values, gain_vec, bias_vec):
    avg_value = lax.optimization_barrier(jnp.mean(values, axis=-1, keepdims=True))
    centred = values - avg_value
    variance = lax.optimization_barrier(jnp.mean(centred * centred, axis=-1, keepdims=True))
    return centred * lax.rsqrt(variance + 1e-05) * gain_vec + bias_vec

def encode(wave_rows, conv0_weight, conv1_weight, norm_gain, norm_bias):
    row_count = wave_rows.shape[0]
    frame_count = (wave_rows.shape[1] - 10) // 10
    sample_blocks = wave_rows.reshape(row_count, 2 * frame_count + 2, 5)
    sample_pairs = jnp.concatenate([sample_blocks[:, :-1], sample_blocks[:, 1:]], axis=2).reshape(-1, 10)
    first_conv = jnp.dot(sample_pairs, conv0_weight, preferred_element_type=jnp.float32)
    first_conv = jax.nn.gelu(layer_norm(first_conv, norm_gain[0], norm_bias[0]), approximate=False).astype(jnp.bfloat16)
    first_conv = first_conv.reshape(row_count, 2 * frame_count + 1, -1)
    conv_taps = jnp.concatenate([first_conv[:, 0:2 * frame_count:2], first_conv[:, 1:2 * frame_count + 1:2], first_conv[:, 2:2 * frame_count + 2:2]], axis=2)
    second_conv = jnp.dot(conv_taps.reshape(row_count * frame_count, -1), conv1_weight, preferred_element_type=jnp.float32)
    return jax.nn.gelu(layer_norm(second_conv, norm_gain[1], norm_bias[1]), approximate=False).astype(jnp.bfloat16)

def reference(waveform, destination, lengths, conv0_weight, conv1_weight, norm_gain, norm_bias, proj_weight, proj_bias, cotangent):
    devices = N_DP * N_FSDP
    row_order = jnp.arange(ROWS_DEV, dtype=jnp.int32)
    targets = destination.reshape(devices, ROWS_DEV)
    same_dest = targets[:, :, None] == targets[:, None, :]
    earlier_rows = row_order[None, :] < row_order[:, None]
    row_rank = lax.optimization_barrier(jnp.sum((same_dest & earlier_rows[None]).astype(jnp.int32), axis=2))
    device_ids = jnp.arange(devices, dtype=jnp.int32)[:, None]
    slot = ((targets * N_FSDP + device_ids % N_FSDP) * N_DP + device_ids // N_FSDP) * CAP + row_rank
    frame_ids = jnp.arange(FR, dtype=jnp.int32)

    def scan_step(totals, step_input):
        wave_rows, row_lengths, slot_index = step_input
        grad_weight, grad_bias, feature_buf = totals
        hidden = encode(wave_rows, conv0_weight, conv1_weight, norm_gain, norm_bias)
        normed = layer_norm(hidden.astype(jnp.float32), norm_gain[2], norm_bias[2]).astype(jnp.bfloat16)
        valid = (10 * frame_ids[None, :] + 20 <= row_lengths[:, None]).reshape(-1, 1)
        frame_mask = valid.astype(jnp.float32)
        projected = jnp.dot(normed, proj_weight, preferred_element_type=jnp.float32) + proj_bias.astype(jnp.float32)
        feats_rows = (projected * frame_mask).astype(jnp.bfloat16).reshape(ROWS_DEV, FR, D_MODEL)
        feature_buf = feature_buf.at[slot_index].set(feats_rows)
        cot_rows = cotangent[slot_index].reshape(ROWS_DEV * FR, D_MODEL)
        grad_out = jnp.where(valid, cot_rows, jnp.zeros_like(cot_rows))
        grad_weight = grad_weight + lax.dot_general(normed, grad_out, (((0,), (0,)), ((), ())), preferred_element_type=jnp.float32)
        grad_bias = grad_bias + lax.optimization_barrier(jnp.sum(grad_out.astype(jnp.float32), axis=0))
        return ((grad_weight, grad_bias, feature_buf), None)
    initial = (jnp.zeros((D_CONV, D_MODEL), jnp.float32), jnp.zeros((D_MODEL,), jnp.float32), jnp.zeros((SLOTS, FR, D_MODEL), cotangent.dtype))
    totals, unused = lax.scan(scan_step, initial, (waveform.reshape(devices, ROWS_DEV, SAMP), lengths.reshape(devices, ROWS_DEV), slot))
    return (totals[2], totals[0].astype(jnp.bfloat16), totals[1].astype(jnp.bfloat16))
```

```python
import functools
import math

import jax
import jax.numpy as jnp
from jax import lax
from jax.experimental import pallas as pl
from jax.experimental.pallas import tpu as pltpu
from jax.sharding import PartitionSpec as P

MESH = pl.DeviceIdType.MESH
F32 = jnp.float32
BF16 = jnp.bfloat16


def gelu(v):
    return 0.5 * v * (1.0 + lax.erf(v * (1.0 / math.sqrt(2.0))))


def norm_rows(values, gain_vec, bias_vec):
    avg = jnp.mean(values, axis=-1, keepdims=True)
    centred = values - avg
    var = jnp.mean(centred * centred, axis=-1, keepdims=True)
    return centred * lax.rsqrt(var + 1e-05) * gain_vec + bias_vec


def dot_t(a, b):
    return lax.dot_general(a, b, (((0,), (0,)), ((), ())), preferred_element_type=F32)


def fused(
    samp, n_dp, n_f, cap, frames,
    data_ref, w0_ref, w1_ref, gain_ref, nbias_ref, pw_ref, pb_ref, cot_ref,
    feat_ref, gw_ref, gb_ref,
    xsend, xrecv, w0p, wfull, pbfull, cotb, normed_ref, masked_ref, mask_ref,
    asend, arecv, gown, bsend, brecv, csend, crecv, gwbuf,
    hsend, hrecv, hsum, hall,
    x_s, x_r, wz_s, wz_r, wp_s, wp_r, wm_s, wm_r, pb_s, pb_r,
    a_s, a_r, b_s, b_r, c_s, c_r, d_s, d_r, e_s, e_r, h_s, h_r, k_s, k_r,
):
    d = lax.axis_index("dp")
    f = lax.axis_index("fsdp")
    core = d % 2
    chip = d // 2
    cx = chip % 2
    cy = chip // 2
    n_chip = n_dp // 2
    depth = pw_ref.shape[0]
    cols = pw_ref.shape[1]
    half = depth // 2
    ch = half // n_chip
    slots = n_dp * cap
    mate = chip * 2 + (1 - core)

    def other(c):
        return ((cy + c // 2) % 2) * 2 + (cx + c % 2) % 2

    def copy(src, dst, s_sem, r_sem, dd, ff):
        return pltpu.make_async_remote_copy(
            src_ref=src, dst_ref=dst, send_sem=s_sem, recv_sem=r_sem,
            device_id=(dd, ff), device_id_type=MESH,
        )

    barrier = pltpu.get_barrier_semaphore()
    for o in range(1, n_dp):
        pl.semaphore_signal(barrier, inc=1, device_id=((d + o) % n_dp, f), device_id_type=MESH)
    for o in range(1, n_f):
        pl.semaphore_signal(barrier, inc=1, device_id=(d, (f + o) % n_f), device_id_type=MESH)

    rows = data_ref.shape[0]
    table = data_ref[...]
    target = table[:, samp + 1 : samp + 2].astype(F32)
    lane = lax.broadcasted_iota(jnp.int32, (rows, 128), 1).astype(F32)
    named = (target == lane).astype(F32)
    tri_r = lax.broadcasted_iota(jnp.int32, (rows, rows), 0)
    tri_c = lax.broadcasted_iota(jnp.int32, (rows, rows), 1)
    earlier = (tri_c < tri_r).astype(F32).astype(BF16)
    before = jnp.dot(earlier, named.astype(BF16), preferred_element_type=F32)
    rank = jnp.sum(before * named, axis=1, keepdims=True)
    place = target * cap + rank
    placing = (place == lane).astype(F32).astype(BF16)
    placed = dot_t(placing, table)[:slots]
    xsend[...] = placed.reshape(n_dp, cap, 128)
    wfull[f] = pw_ref[...]
    pbfull[f] = jnp.broadcast_to(pb_ref[...].astype(F32), (8, cols))
    pl.semaphore_wait(barrier, n_dp + n_f - 2)

    x_cp = []
    for o in range(1, n_dp):
        p = (d + o) % n_dp
        x_cp.append(copy(xsend.at[p], xrecv.at[d], x_s.at[o], x_r.at[o], p, f))
        x_cp[-1].start()
    mine = core * half + chip * ch
    z_cp, pb_cp = [], []
    for o in range(1, n_f):
        p = (f + o) % n_f
        z_cp.append(copy(
            wfull.at[f, pl.ds(mine, ch)], wfull.at[f, pl.ds(mine, ch)],
            wz_s.at[o], wz_r.at[o], d, p))
        z_cp[-1].start()
        pb_cp.append(copy(pbfull.at[f], pbfull.at[f], pb_s.at[o], pb_r.at[o], d, p))
        pb_cp[-1].start()
    xrecv[d] = xsend[d]
    w0p[...] = jnp.zeros_like(w0p)
    w0p[0 : w0_ref.shape[0], :] = w0_ref[...]
    for b in range(n_f):
        cotb[b] = cot_ref[:, b * cols : (b + 1) * cols]
    for o in range(1, n_dp):
        q = (d + n_dp - o) % n_dp
        copy(xsend.at[q], xrecv.at[q], x_s.at[o], x_r.at[o], q, f).wait_recv()

    x = xrecv[...].reshape(slots, 128)
    length = x[:, samp : samp + 1]
    first = []
    for t in range(2 * frames + 1):
        xt = x if t == 0 else pltpu.roll(x, 128 - 5 * t, axis=1)
        v = jnp.dot(xt.astype(BF16), w0p[...], preferred_element_type=F32)
        first.append(gelu(norm_rows(v, gain_ref[0:1], nbias_ref[0:1])).astype(BF16))

    p_cp = []
    for o in range(1, n_f):
        q = (f + n_f - o) % n_f
        part = wfull.at[q, pl.ds(mine, ch)]
        copy(part, part, wz_s.at[o], wz_r.at[o], d, q).wait_recv()
        for c in range(1, n_chip):
            i = o * n_chip + c
            p_cp.append(copy(part, part, wp_s.at[i], wp_r.at[i], other(c) * 2 + core, f))
            p_cp[-1].start()

    normed, masked, masks = [], [], []
    for j in range(frames):
        taps = jnp.concatenate(first[2 * j : 2 * j + 3], axis=1)
        v = jnp.dot(taps, w1_ref[...], preferred_element_type=F32)
        hid = gelu(norm_rows(v, gain_ref[1:2], nbias_ref[1:2])).astype(BF16).astype(F32)
        nj = norm_rows(hid, gain_ref[2:3], nbias_ref[2:3]).astype(BF16)
        mj = (length >= 10.0 * j + 20.0).astype(F32)
        normed.append(nj)
        masks.append(jnp.broadcast_to(mj, (slots, 128)).astype(BF16))
    total = slots * frames
    pr = lax.broadcasted_iota(jnp.int32, (total, total), 0)
    pc = lax.broadcasted_iota(jnp.int32, (total, total), 1)
    perm = ((pr % frames) * slots + pr // frames == pc).astype(F32).astype(BF16)
    nrm = jnp.dot(perm, jnp.concatenate(normed, axis=0), preferred_element_type=F32)
    msk = jnp.dot(perm, jnp.concatenate(masks, axis=0), preferred_element_type=F32)
    normed_ref[...] = nrm.astype(BF16)
    masked_ref[...] = (nrm * msk[:, 0:1]).astype(BF16)
    mask_ref[...] = msk

    order = [o % n_f for o in range(1, n_f + 1)]
    a_cp = []
    theirs = masked_ref[:, pl.ds(pl.multiple_of((1 - core) * half, half), half)]
    for o in order:
        b = (f + o) % n_f
        asend[o] = dot_t(theirs, cotb[b]).astype(BF16)
        a_cp.append(copy(asend.at[o], arecv.at[o], a_s.at[o], a_r.at[o], mate, f))
        a_cp[-1].start()
    ours = masked_ref[:, pl.ds(pl.multiple_of(core * half, half), half)]
    for o in order:
        b = (f + o) % n_f
        gown[o] = dot_t(ours, cotb[b])
    h_cp = []
    ones = mask_ref[...].astype(BF16)
    for o in order:
        b = (f + o) % n_f
        hsend[o] = dot_t(ones, cotb[b])[0:8]
        if o:
            h_cp.append(copy(hsend.at[o], hrecv.at[o], h_s.at[o], h_r.at[o], d, b))
            h_cp[-1].start()

    b_cp = []
    for o in order:
        copy(asend.at[o], arecv.at[o], a_s.at[o], a_r.at[o], mate, f).wait_recv()
        both = gown[o] + arecv[o].astype(F32)
        gown[o] = both
        bsend[o] = both.astype(BF16)
        for c in range(1, n_chip):
            to = other(c)
            i = o * n_chip + c
            b_cp.append(copy(
                bsend.at[o, pl.ds(to * ch, ch)], brecv.at[i],
                b_s.at[i], b_r.at[i], to * 2 + core, f))
            b_cp[-1].start()

    m_cp = []
    for o in range(1, n_f):
        q = (f + n_f - o) % n_f
        for c in range(1, n_chip):
            i = o * n_chip + c
            theirs_at = core * half + other(c) * ch
            part = wfull.at[q, pl.ds(theirs_at, ch)]
            copy(part, part, wp_s.at[i], wp_r.at[i], other(c) * 2 + core, f).wait_recv()
        block = wfull.at[q, pl.ds(core * half, half)]
        m_cp.append(copy(block, block, wm_s.at[o], wm_r.at[o], mate, f))
        m_cp[-1].start()
        copy(pbfull.at[q], pbfull.at[q], pb_s.at[o], pb_r.at[o], d, q).wait_recv()
    for o in range(1, n_f):
        q = (f + n_f - o) % n_f
        block = wfull.at[q, pl.ds((1 - core) * half, half)]
        copy(block, block, wm_s.at[o], wm_r.at[o], mate, f).wait_recv()
    for b in range(n_f):
        v = jnp.dot(normed_ref[...], wfull[b], preferred_element_type=F32) + pbfull[b][0:1]
        feat_ref[:, b * cols : (b + 1) * cols] = (v * mask_ref[:, 0:1]).astype(BF16)

    c_cp = []
    own = None
    for o in order:
        part = gown[o, pl.ds(chip * ch, ch), :]
        for c in range(1, n_chip):
            i = o * n_chip + c
            copy(brecv.at[i], brecv.at[i], b_s.at[i], b_r.at[i], other(c) * 2 + core, f).wait_recv()
            part = part + brecv[i].astype(F32)
        if o:
            csend[o] = part.astype(BF16)
            c_cp.append(copy(csend.at[o], crecv.at[o], c_s.at[o], c_r.at[o], d, (f + o) % n_f))
            c_cp[-1].start()
        else:
            own = part
    hown = hsend[0]
    for o in range(1, n_f):
        q = (f + n_f - o) % n_f
        copy(hsend.at[o], hrecv.at[o], h_s.at[o], h_r.at[o], d, q).wait_recv()
        hown = hown + hrecv[o]
    hsum[...] = hown
    k_cp = []
    for o in range(1, n_dp):
        k_cp.append(copy(hsum, hall.at[o], k_s.at[o], k_r.at[o], (d + o) % n_dp, f))
        k_cp[-1].start()
    for o in range(1, n_f):
        q = (f + n_f - o) % n_f
        copy(csend.at[o], crecv.at[o], c_s.at[o], c_r.at[o], d, q).wait_recv()
        own = own + crecv[o].astype(F32)
    gwbuf[pl.ds(mine, ch), :] = own.astype(BF16)

    d_cp = []
    src = gwbuf.at[pl.ds(mine, ch)]
    for c in range(1, n_chip):
        d_cp.append(copy(src, src, d_s.at[c], d_r.at[c], other(c) * 2 + core, f))
        d_cp[-1].start()
    e_cp = [copy(src, src, e_s.at[0], e_r.at[0], mate, f)]
    e_cp[0].start()
    for c in range(1, n_chip):
        part = gwbuf.at[pl.ds(core * half + other(c) * ch, ch)]
        copy(part, part, d_s.at[c], d_r.at[c], other(c) * 2 + core, f).wait_recv()
        e_cp.append(copy(part, part, e_s.at[c], e_r.at[c], mate, f))
        e_cp[-1].start()
    for o in range(1, n_dp):
        copy(hsum, hall.at[o], k_s.at[o], k_r.at[o], (d + n_dp - o) % n_dp, f).wait_recv()
        hown = hown + hall[o]
    gb_ref[...] = hown[0:1].astype(BF16)
    for c in range(n_chip):
        at = other(c) if c else chip
        part = gwbuf.at[pl.ds((1 - core) * half + at * ch, ch)]
        copy(part, part, e_s.at[c], e_r.at[c], mate, f).wait_recv()
    gw_ref[...] = gwbuf[...]
    for one in x_cp + z_cp + pb_cp + p_cp + m_cp + a_cp + h_cp + b_cp + c_cp + k_cp + d_cp + e_cp:
        one.wait_send()


def local_fused(
    waveform, destination, lengths, conv0_weight, conv1_weight,
    norm_gain, norm_bias, proj_weight, proj_bias, cotangent,
):
    n_dp, n_f = lax.axis_size("dp"), lax.axis_size("fsdp")
    rows, samp = waveform.shape
    slots, frames, width = cotangent.shape
    cap = slots // n_dp
    depth, cols = proj_weight.shape
    n_chip, half = n_dp // 2, depth // 2
    ch = half // n_chip
    total = slots * frames
    data = jnp.concatenate(
        [waveform, lengths[:, None].astype(BF16), destination.astype(BF16),
         jnp.zeros((rows, 128 - samp - 2), BF16)], axis=1)
    vmem = pl.BlockSpec(memory_space=pltpu.VMEM)
    dma = lambda n: pltpu.SemaphoreType.DMA((n,))
    nc = n_f * n_chip
    feats, gw, gb = pl.pallas_call(
        functools.partial(fused, samp, n_dp, n_f, cap, frames),
        out_shape=(
            jax.ShapeDtypeStruct((total, width), BF16),
            jax.ShapeDtypeStruct((depth, cols), BF16),
            jax.ShapeDtypeStruct((1, cols), BF16),
        ),
        in_specs=[vmem] * 8,
        out_specs=(vmem,) * 3,
        scratch_shapes=[
            pltpu.VMEM((n_dp, cap, 128), F32),
            pltpu.VMEM((n_dp, cap, 128), F32),
            pltpu.VMEM((128, depth), BF16),
            pltpu.VMEM((n_f, depth, cols), BF16),
            pltpu.VMEM((n_f, 8, cols), F32),
            pltpu.VMEM((n_f, total, cols), BF16),
            pltpu.VMEM((total, depth), BF16),
            pltpu.VMEM((total, depth), BF16),
            pltpu.VMEM((total, 128), F32),
            pltpu.VMEM((n_f, half, cols), BF16),
            pltpu.VMEM((n_f, half, cols), BF16),
            pltpu.VMEM((n_f, half, cols), F32),
            pltpu.VMEM((n_f, half, cols), BF16),
            pltpu.VMEM((nc, ch, cols), BF16),
            pltpu.VMEM((n_f, ch, cols), BF16),
            pltpu.VMEM((n_f, ch, cols), BF16),
            pltpu.VMEM((depth, cols), BF16),
            pltpu.VMEM((n_f, 8, cols), F32),
            pltpu.VMEM((n_f, 8, cols), F32),
            pltpu.VMEM((8, cols), F32),
            pltpu.VMEM((n_dp, 8, cols), F32),
            dma(n_dp), dma(n_dp), dma(n_f), dma(n_f), dma(nc), dma(nc),
            dma(n_f), dma(n_f), dma(n_f), dma(n_f),
            dma(n_f), dma(n_f), dma(nc), dma(nc), dma(n_f), dma(n_f),
            dma(n_chip), dma(n_chip), dma(n_chip), dma(n_chip),
            dma(n_f), dma(n_f), dma(n_dp), dma(n_dp),
        ],
        compiler_params=pltpu.CompilerParams(
            collective_id=0, has_side_effects=True, vmem_limit_bytes=48 * 1024 * 1024),
        cost_estimate=pl.CostEstimate(
            flops=2 * total * depth * (3 * depth + 2 * width),
            bytes_accessed=8 * depth * width, transcendentals=13 * slots * depth),
    )(data, conv0_weight, conv1_weight, norm_gain, norm_bias, proj_weight,
      proj_bias[None, :], cotangent.reshape(total, width))
    return feats.reshape(slots, frames, width), gw, gb[0]


def layer_norm(values, gain_vec, bias_vec):
    avg_value = jnp.mean(values, axis=-1, keepdims=True)
    centred = values - avg_value
    variance = jnp.mean(centred * centred, axis=-1, keepdims=True)
    return centred * lax.rsqrt(variance + 1e-05) * gain_vec + bias_vec


def encode(wave_rows, conv0_weight, conv1_weight, norm_gain, norm_bias):
    row_count = wave_rows.shape[0]
    frame_count = (wave_rows.shape[1] - 10) // 10
    sample_blocks = wave_rows.reshape(row_count, 2 * frame_count + 2, 5)
    sample_pairs = jnp.concatenate([sample_blocks[:, :-1], sample_blocks[:, 1:]], axis=2).reshape(
        -1, 10
    )
    first_conv = jnp.dot(sample_pairs, conv0_weight, preferred_element_type=jnp.float32)
    first_conv = jax.nn.gelu(
        layer_norm(first_conv, norm_gain[0], norm_bias[0]), approximate=False
    ).astype(jnp.bfloat16)
    first_conv = first_conv.reshape(row_count, 2 * frame_count + 1, -1)
    conv_taps = jnp.concatenate(
        [
            first_conv[:, 0 : 2 * frame_count : 2],
            first_conv[:, 1 : 2 * frame_count + 1 : 2],
            first_conv[:, 2 : 2 * frame_count + 2 : 2],
        ],
        axis=2,
    )
    second_conv = jnp.dot(
        conv_taps.reshape(row_count * frame_count, -1),
        conv1_weight,
        preferred_element_type=jnp.float32,
    )
    return jax.nn.gelu(
        layer_norm(second_conv, norm_gain[1], norm_bias[1]), approximate=False
    ).astype(jnp.bfloat16)


def local(
    waveform,
    destination,
    lengths,
    conv0_weight,
    conv1_weight,
    norm_gain,
    norm_bias,
    proj_weight,
    proj_bias,
    cotangent,
):
    dp_size = lax.axis_size("dp")
    row_count = waveform.shape[0]
    slot_count = cotangent.shape[0]
    frame_count = cotangent.shape[1]
    slot_cap = slot_count // dp_size
    weights, biases = (
        lax.all_gather(proj_weight, "fsdp", axis=1, tiled=True),
        lax.all_gather(proj_bias, "fsdp", axis=0, tiled=True),
    )
    targets = destination[:, 0]
    row_order = jnp.arange(row_count, dtype=jnp.int32)
    same_dest = targets[:, None] == targets[None, :]
    earlier_rows = row_order[None, :] < row_order[:, None]
    row_rank = jnp.sum((same_dest & earlier_rows).astype(jnp.int32), axis=1)
    position = targets * slot_cap + row_rank
    placing = position[None, :] == jnp.arange(slot_count, dtype=jnp.int32)[:, None]
    slot_length = jnp.sum(jnp.where(placing, lengths[None, :], 0), axis=1)
    placing_matrix = placing.astype(jnp.bfloat16)
    slot_wave = jnp.dot(placing_matrix, waveform, preferred_element_type=jnp.float32).astype(
        jnp.bfloat16
    )
    got_wave, got_length = (
        lax.all_to_all(
            slot_wave.reshape(dp_size, slot_cap, -1), "dp", split_axis=0, concat_axis=0, tiled=True
        ),
        lax.all_to_all(
            slot_length.reshape(dp_size, slot_cap), "dp", split_axis=0, concat_axis=0, tiled=True
        ),
    )
    hidden = encode(
        got_wave.reshape(slot_count, -1), conv0_weight, conv1_weight, norm_gain, norm_bias
    )
    got_length = got_length.reshape(slot_count)
    normed = layer_norm(hidden.astype(jnp.float32), norm_gain[2], norm_bias[2]).astype(jnp.bfloat16)
    frame_ids = jnp.arange(frame_count, dtype=jnp.int32)
    valid = (10 * frame_ids[None, :] + 20 <= got_length[:, None]).reshape(-1, 1)
    frame_mask = valid.astype(jnp.float32)
    projected = jnp.dot(normed, weights, preferred_element_type=jnp.float32) + biases.astype(
        jnp.float32
    )
    features = (projected * frame_mask).astype(jnp.bfloat16).reshape(slot_count, frame_count, -1)
    cot_rows = cotangent.reshape(slot_count * frame_count, -1)
    grad_out = jnp.where(valid, cot_rows, jnp.zeros_like(cot_rows))
    weight_term = lax.dot_general(
        normed, grad_out, (((0,), (0,)), ((), ())), preferred_element_type=jnp.float32
    )
    bias_term = jnp.sum(grad_out, axis=0, dtype=jnp.float32)
    part_weight, part_bias = (
        lax.psum_scatter(weight_term, "fsdp", scatter_dimension=1, tiled=True),
        lax.psum_scatter(bias_term, "fsdp", scatter_dimension=0, tiled=True),
    )
    grad_weight, grad_bias = lax.psum((part_weight, part_bias), "dp")
    return (features, grad_weight.astype(jnp.bfloat16), grad_bias.astype(jnp.bfloat16))


def solution(mesh):
    in_specs = (
        P(("dp", "fsdp"), None),
        P(("dp", "fsdp"), None),
        P(("dp", "fsdp")),
        P(),
        P(),
        P(),
        P(),
        P(None, "fsdp"),
        P("fsdp"),
        P(("dp", "fsdp"), None, None),
    )
    out_specs = (P(("dp", "fsdp"), None, None), P(None, "fsdp"), P("fsdp"))
    body = local_fused if (mesh.shape["dp"], mesh.shape["fsdp"]) == (8, 4) else local
    return jax.shard_map(body, mesh=mesh, in_specs=in_specs, out_specs=out_specs, check_vma=False)
```

```python
import functools
import math

import jax
import jax.numpy as jnp
from jax import lax
from jax.experimental import pallas as pl
from jax.experimental.pallas import tpu as pltpu
from jax.sharding import PartitionSpec as P

MESH = pl.DeviceIdType.MESH
F32 = jnp.float32
BF16 = jnp.bfloat16


def gelu(v):
    return 0.5 * v * (1.0 + lax.erf(v * (1.0 / math.sqrt(2.0))))


def norm_rows(values, gain_vec, bias_vec):
    avg = jnp.mean(values, axis=-1, keepdims=True)
    centred = values - avg
    var = jnp.mean(centred * centred, axis=-1, keepdims=True)
    return centred * lax.rsqrt(var + 1e-05) * gain_vec + bias_vec


def dot_t(a, b):
    return lax.dot_general(a, b, (((0,), (0,)), ((), ())), preferred_element_type=F32)


def fused(
    samp, n_dp, n_f, cap, frames,
    wave_ref, dest_ref, len_ref, w0_ref, w1_hbm, gain_ref, nbias_ref, pw_ref, pb_ref, cot_ref,
    feat_ref, gw_ref, gb_ref,
    w1_ref, w1_sem, table_ref, xsend, xrecv, w0p, wfull, pbfull, cotb, normed_ref, masked_ref, mask_ref,
    asend, arecv, gown, bsend, brecv, csend, crecv, gwbuf,
    hsend, hrecv, hsum, hall,
    x_s, x_r, wz_s, wz_r, wp_s, wp_r, wm_s, wm_r, pb_s, pb_r,
    a_s, a_r, b_s, b_r, c_s, c_r, d_s, d_r, e_s, e_r, h_s, h_r, k_s, k_r,
):
    d = lax.axis_index("dp")
    f = lax.axis_index("fsdp")
    core = d % 2
    chip = d // 2
    cx = chip % 2
    cy = chip // 2
    n_chip = n_dp // 2
    cols, depth = pw_ref.shape
    half = depth // 2
    ch = half // n_chip
    slots = n_dp * cap
    mate = chip * 2 + (1 - core)

    def other(c):
        return ((cy + c // 2) % 2) * 2 + (cx + c % 2) % 2

    def copy(src, dst, s_sem, r_sem, dd, ff):
        return pltpu.make_async_remote_copy(
            src_ref=src, dst_ref=dst, send_sem=s_sem, recv_sem=r_sem,
            device_id=(dd, ff), device_id_type=MESH,
        )

    w1_cp = pltpu.make_async_copy(w1_hbm, w1_ref, w1_sem)
    w1_cp.start()
    barrier = pltpu.get_barrier_semaphore()
    for o in range(1, n_dp):
        pl.semaphore_signal(barrier, inc=1, device_id=((d + o) % n_dp, f), device_id_type=MESH)
    for o in range(1, n_f):
        pl.semaphore_signal(barrier, inc=1, device_id=(d, (f + o) % n_f), device_id_type=MESH)

    rows = wave_ref.shape[0]
    tri_r = lax.broadcasted_iota(jnp.int32, (rows, rows), 0)
    tri_c = lax.broadcasted_iota(jnp.int32, (rows, rows), 1)
    lane = lax.broadcasted_iota(jnp.int32, (rows, 128), 1)
    spread = jnp.broadcast_to(len_ref[...].astype(F32), (rows, rows))
    span = jnp.sum(jnp.where(tri_r == tri_c, spread, 0.0), axis=1, keepdims=True)
    table_ref[...] = jnp.where(lane == samp, span, 0.0).astype(BF16)
    table_ref[:, 0:samp] = wave_ref[...]
    table = table_ref[...]
    lane = lane.astype(F32)
    target = dest_ref[...].astype(F32)
    named = (target == lane).astype(F32)
    earlier = (tri_c < tri_r).astype(F32).astype(BF16)
    before = jnp.dot(earlier, named.astype(BF16), preferred_element_type=F32)
    rank = jnp.sum(before * named, axis=1, keepdims=True)
    place = target * cap + rank
    placing = (place == lane).astype(F32).astype(BF16)
    placed = dot_t(placing, table)[:slots]
    xsend[...] = placed.reshape(n_dp, cap, 128)
    eye_r = lax.broadcasted_iota(jnp.int32, (depth, depth), 0)
    eye_c = lax.broadcasted_iota(jnp.int32, (depth, depth), 1)
    eye = (eye_r == eye_c).astype(F32).astype(BF16)
    wfull[f] = lax.dot_general(
        eye, pw_ref[...], (((1,), (1,)), ((), ())), preferred_element_type=F32).astype(BF16)
    pbfull[f] = jnp.broadcast_to(pb_ref[...].astype(F32)[None, :], (8, cols))
    pl.semaphore_wait(barrier, n_dp + n_f - 2)

    x_cp = []
    for o in range(1, n_dp):
        p = (d + o) % n_dp
        x_cp.append(copy(xsend.at[p], xrecv.at[d], x_s.at[o], x_r.at[o], p, f))
        x_cp[-1].start()
    mine = core * half + chip * ch
    z_cp, pb_cp = [], []
    for o in range(1, n_f):
        p = (f + o) % n_f
        z_cp.append(copy(
            wfull.at[f, pl.ds(mine, ch)], wfull.at[f, pl.ds(mine, ch)],
            wz_s.at[o], wz_r.at[o], d, p))
        z_cp[-1].start()
        pb_cp.append(copy(pbfull.at[f], pbfull.at[f], pb_s.at[o], pb_r.at[o], d, p))
        pb_cp[-1].start()
    xrecv[d] = xsend[d]
    w0p[...] = jnp.zeros_like(w0p)
    w0p[0 : w0_ref.shape[0], :] = w0_ref[...]
    for b in range(n_f):
        cotb[b] = cot_ref[:, b * cols : (b + 1) * cols]
    for o in range(1, n_dp):
        q = (d + n_dp - o) % n_dp
        copy(xsend.at[q], xrecv.at[q], x_s.at[o], x_r.at[o], q, f).wait_recv()

    x = xrecv[...].reshape(slots, 128)
    length = x[:, samp : samp + 1]
    first, p_cp = [], []
    for t in range(2 * frames + 1):
        xt = x if t == 0 else pltpu.roll(x, 128 - 5 * t, axis=1)
        v = jnp.dot(xt.astype(BF16), w0p[...], preferred_element_type=F32)
        first.append(gelu(norm_rows(v, gain_ref[0:1], nbias_ref[0:1])).astype(BF16))
        for o in range(1, n_f):
            if t != (2 * frames + 1) * o // n_f:
                continue
            q = (f + n_f - o) % n_f
            part = wfull.at[q, pl.ds(mine, ch)]
            copy(part, part, wz_s.at[o], wz_r.at[o], d, q).wait_recv()
            for c in range(1, n_chip):
                i = o * n_chip + c
                p_cp.append(copy(part, part, wp_s.at[i], wp_r.at[i], other(c) * 2 + core, f))
                p_cp[-1].start()

    w1_cp.wait()
    normed, masked, masks = [], [], []
    for j in range(frames):
        taps = jnp.concatenate(first[2 * j : 2 * j + 3], axis=1)
        v = jnp.dot(taps, w1_ref[...], preferred_element_type=F32)
        hid = gelu(norm_rows(v, gain_ref[1:2], nbias_ref[1:2])).astype(BF16).astype(F32)
        nj = norm_rows(hid, gain_ref[2:3], nbias_ref[2:3]).astype(BF16)
        mj = (length >= 10.0 * j + 20.0).astype(F32)
        normed.append(nj)
        masks.append(jnp.broadcast_to(mj, (slots, 128)).astype(BF16))
    total = slots * frames
    pr = lax.broadcasted_iota(jnp.int32, (total, total), 0)
    pc = lax.broadcasted_iota(jnp.int32, (total, total), 1)
    perm = ((pr % frames) * slots + pr // frames == pc).astype(F32).astype(BF16)
    nrm = jnp.dot(perm, jnp.concatenate(normed, axis=0), preferred_element_type=F32)
    msk = jnp.dot(perm, jnp.concatenate(masks, axis=0), preferred_element_type=F32)
    normed_ref[...] = nrm.astype(BF16)
    masked_ref[...] = (nrm * msk[:, 0:1]).astype(BF16)
    mask_ref[...] = msk

    order = [o % n_f for o in range(1, n_f + 1)]
    a_cp = []
    theirs = masked_ref[:, pl.ds(pl.multiple_of((1 - core) * half, half), half)]
    for o in order:
        b = (f + o) % n_f
        asend[o] = dot_t(theirs, cotb[b]).astype(BF16)
        a_cp.append(copy(asend.at[o], arecv.at[o], a_s.at[o], a_r.at[o], mate, f))
        a_cp[-1].start()
    ours = masked_ref[:, pl.ds(pl.multiple_of(core * half, half), half)]
    for o in order:
        b = (f + o) % n_f
        gown[o] = dot_t(ours, cotb[b])
    h_cp = []
    ones = mask_ref[...].astype(BF16)
    for o in order:
        b = (f + o) % n_f
        hsend[o] = dot_t(ones, cotb[b])[0:8]
        if o:
            h_cp.append(copy(hsend.at[o], hrecv.at[o], h_s.at[o], h_r.at[o], d, b))
            h_cp[-1].start()

    b_cp = []
    for o in order:
        copy(asend.at[o], arecv.at[o], a_s.at[o], a_r.at[o], mate, f).wait_recv()
        both = gown[o] + arecv[o].astype(F32)
        gown[o] = both
        bsend[o] = both.astype(BF16)
        for c in range(1, n_chip):
            to = other(c)
            i = o * n_chip + c
            b_cp.append(copy(
                bsend.at[o, pl.ds(to * ch, ch)], brecv.at[i],
                b_s.at[i], b_r.at[i], to * 2 + core, f))
            b_cp[-1].start()

    m_cp = []
    for o in range(1, n_f):
        q = (f + n_f - o) % n_f
        for c in range(1, n_chip):
            i = o * n_chip + c
            theirs_at = core * half + other(c) * ch
            part = wfull.at[q, pl.ds(theirs_at, ch)]
            copy(part, part, wp_s.at[i], wp_r.at[i], other(c) * 2 + core, f).wait_recv()
        block = wfull.at[q, pl.ds(core * half, half)]
        m_cp.append(copy(block, block, wm_s.at[o], wm_r.at[o], mate, f))
        m_cp[-1].start()
        copy(pbfull.at[q], pbfull.at[q], pb_s.at[o], pb_r.at[o], d, q).wait_recv()
    for o in range(1, n_f):
        q = (f + n_f - o) % n_f
        block = wfull.at[q, pl.ds((1 - core) * half, half)]
        copy(block, block, wm_s.at[o], wm_r.at[o], mate, f).wait_recv()
    for b in range(n_f):
        v = jnp.dot(normed_ref[...], wfull[b], preferred_element_type=F32) + pbfull[b][0:1]
        feat_ref[:, b * cols : (b + 1) * cols] = (v * mask_ref[:, 0:1]).astype(BF16)

    c_cp = []
    own = None
    for o in order:
        part = gown[o, pl.ds(chip * ch, ch), :]
        for c in range(1, n_chip):
            i = o * n_chip + c
            copy(brecv.at[i], brecv.at[i], b_s.at[i], b_r.at[i], other(c) * 2 + core, f).wait_recv()
            part = part + brecv[i].astype(F32)
        if o:
            csend[o] = part.astype(BF16)
            c_cp.append(copy(csend.at[o], crecv.at[o], c_s.at[o], c_r.at[o], d, (f + o) % n_f))
            c_cp[-1].start()
        else:
            own = part
    hown = hsend[0]
    for o in range(1, n_f):
        q = (f + n_f - o) % n_f
        copy(hsend.at[o], hrecv.at[o], h_s.at[o], h_r.at[o], d, q).wait_recv()
        hown = hown + hrecv[o]
    hsum[...] = hown
    k_cp = []
    for o in range(1, n_dp):
        k_cp.append(copy(hsum, hall.at[o], k_s.at[o], k_r.at[o], (d + o) % n_dp, f))
        k_cp[-1].start()
    for o in range(1, n_f):
        q = (f + n_f - o) % n_f
        copy(csend.at[o], crecv.at[o], c_s.at[o], c_r.at[o], d, q).wait_recv()
        own = own + crecv[o].astype(F32)
    gwbuf[pl.ds(mine, ch), :] = own.astype(BF16)

    d_cp = []
    src = gwbuf.at[pl.ds(mine, ch)]
    for c in range(1, n_chip):
        d_cp.append(copy(src, src, d_s.at[c], d_r.at[c], other(c) * 2 + core, f))
        d_cp[-1].start()
    e_cp = [copy(src, src, e_s.at[0], e_r.at[0], mate, f)]
    e_cp[0].start()
    for c in range(1, n_chip):
        part = gwbuf.at[pl.ds(core * half + other(c) * ch, ch)]
        copy(part, part, d_s.at[c], d_r.at[c], other(c) * 2 + core, f).wait_recv()
        e_cp.append(copy(part, part, e_s.at[c], e_r.at[c], mate, f))
        e_cp[-1].start()
    for o in range(1, n_dp):
        copy(hsum, hall.at[o], k_s.at[o], k_r.at[o], (d + n_dp - o) % n_dp, f).wait_recv()
        hown = hown + hall[o]
    gb_ref[...] = hown[0].astype(BF16)
    for c in range(n_chip):
        at = other(c) if c else chip
        part = gwbuf.at[pl.ds((1 - core) * half + at * ch, ch)]
        copy(part, part, e_s.at[c], e_r.at[c], mate, f).wait_recv()
    gw_ref[...] = dot_t(gwbuf[...], eye).astype(BF16)
    for one in x_cp + z_cp + pb_cp + p_cp + m_cp + a_cp + h_cp + b_cp + c_cp + k_cp + d_cp + e_cp:
        one.wait_send()


def local_fused(
    waveform, destination, lengths, conv0_weight, conv1_weight,
    norm_gain, norm_bias, proj_weight, proj_bias, cotangent,
):
    n_dp, n_f = lax.axis_size("dp"), lax.axis_size("fsdp")
    rows, samp = waveform.shape
    slots, frames, width = cotangent.shape
    cap = slots // n_dp
    depth, cols = proj_weight.shape
    n_chip, half = n_dp // 2, depth // 2
    ch = half // n_chip
    total = slots * frames
    vmem = pl.BlockSpec(memory_space=pltpu.VMEM)
    hbm = pl.BlockSpec(memory_space=pltpu.HBM)
    dma = lambda n: pltpu.SemaphoreType.DMA((n,))
    nc = n_f * n_chip
    feats, gw, gb = pl.pallas_call(
        functools.partial(fused, samp, n_dp, n_f, cap, frames),
        out_shape=(
            jax.ShapeDtypeStruct((total, width), BF16),
            jax.ShapeDtypeStruct((cols, depth), BF16),
            jax.ShapeDtypeStruct((cols,), BF16),
        ),
        in_specs=[vmem] * 4 + [hbm] + [vmem] * 5,
        out_specs=(vmem,) * 3,
        scratch_shapes=[
            pltpu.VMEM(conv1_weight.shape, BF16),
            pltpu.SemaphoreType.DMA,
            pltpu.VMEM((rows, 128), BF16),
            pltpu.VMEM((n_dp, cap, 128), F32),
            pltpu.VMEM((n_dp, cap, 128), F32),
            pltpu.VMEM((128, depth), BF16),
            pltpu.VMEM((n_f, depth, cols), BF16),
            pltpu.VMEM((n_f, 8, cols), F32),
            pltpu.VMEM((n_f, total, cols), BF16),
            pltpu.VMEM((total, depth), BF16),
            pltpu.VMEM((total, depth), BF16),
            pltpu.VMEM((total, 128), F32),
            pltpu.VMEM((n_f, half, cols), BF16),
            pltpu.VMEM((n_f, half, cols), BF16),
            pltpu.VMEM((n_f, half, cols), F32),
            pltpu.VMEM((n_f, half, cols), BF16),
            pltpu.VMEM((nc, ch, cols), BF16),
            pltpu.VMEM((n_f, ch, cols), BF16),
            pltpu.VMEM((n_f, ch, cols), BF16),
            pltpu.VMEM((depth, cols), BF16),
            pltpu.VMEM((n_f, 8, cols), F32),
            pltpu.VMEM((n_f, 8, cols), F32),
            pltpu.VMEM((8, cols), F32),
            pltpu.VMEM((n_dp, 8, cols), F32),
            dma(n_dp), dma(n_dp), dma(n_f), dma(n_f), dma(nc), dma(nc),
            dma(n_f), dma(n_f), dma(n_f), dma(n_f),
            dma(n_f), dma(n_f), dma(nc), dma(nc), dma(n_f), dma(n_f),
            dma(n_chip), dma(n_chip), dma(n_chip), dma(n_chip),
            dma(n_f), dma(n_f), dma(n_dp), dma(n_dp),
        ],
        compiler_params=pltpu.CompilerParams(
            collective_id=0, has_side_effects=True, vmem_limit_bytes=48 * 1024 * 1024),
        cost_estimate=pl.CostEstimate(
            flops=2 * total * depth * (3 * depth + 2 * width),
            bytes_accessed=8 * depth * width, transcendentals=13 * slots * depth),
    )(waveform, destination, lengths[None, :], conv0_weight, conv1_weight,
      norm_gain, norm_bias, proj_weight.T, proj_bias, cotangent.reshape(total, width))
    return feats.reshape(slots, frames, width), gw.T, gb


def layer_norm(values, gain_vec, bias_vec):
    avg_value = jnp.mean(values, axis=-1, keepdims=True)
    centred = values - avg_value
    variance = jnp.mean(centred * centred, axis=-1, keepdims=True)
    return centred * lax.rsqrt(variance + 1e-05) * gain_vec + bias_vec


def encode(wave_rows, conv0_weight, conv1_weight, norm_gain, norm_bias):
    row_count = wave_rows.shape[0]
    frame_count = (wave_rows.shape[1] - 10) // 10
    sample_blocks = wave_rows.reshape(row_count, 2 * frame_count + 2, 5)
    sample_pairs = jnp.concatenate([sample_blocks[:, :-1], sample_blocks[:, 1:]], axis=2).reshape(
        -1, 10
    )
    first_conv = jnp.dot(sample_pairs, conv0_weight, preferred_element_type=jnp.float32)
    first_conv = jax.nn.gelu(
        layer_norm(first_conv, norm_gain[0], norm_bias[0]), approximate=False
    ).astype(jnp.bfloat16)
    first_conv = first_conv.reshape(row_count, 2 * frame_count + 1, -1)
    conv_taps = jnp.concatenate(
        [
            first_conv[:, 0 : 2 * frame_count : 2],
            first_conv[:, 1 : 2 * frame_count + 1 : 2],
            first_conv[:, 2 : 2 * frame_count + 2 : 2],
        ],
        axis=2,
    )
    second_conv = jnp.dot(
        conv_taps.reshape(row_count * frame_count, -1),
        conv1_weight,
        preferred_element_type=jnp.float32,
    )
    return jax.nn.gelu(
        layer_norm(second_conv, norm_gain[1], norm_bias[1]), approximate=False
    ).astype(jnp.bfloat16)


def local(
    waveform,
    destination,
    lengths,
    conv0_weight,
    conv1_weight,
    norm_gain,
    norm_bias,
    proj_weight,
    proj_bias,
    cotangent,
):
    dp_size = lax.axis_size("dp")
    row_count = waveform.shape[0]
    slot_count = cotangent.shape[0]
    frame_count = cotangent.shape[1]
    slot_cap = slot_count // dp_size
    weights, biases = (
        lax.all_gather(proj_weight, "fsdp", axis=1, tiled=True),
        lax.all_gather(proj_bias, "fsdp", axis=0, tiled=True),
    )
    targets = destination[:, 0]
    row_order = jnp.arange(row_count, dtype=jnp.int32)
    same_dest = targets[:, None] == targets[None, :]
    earlier_rows = row_order[None, :] < row_order[:, None]
    row_rank = jnp.sum((same_dest & earlier_rows).astype(jnp.int32), axis=1)
    position = targets * slot_cap + row_rank
    placing = position[None, :] == jnp.arange(slot_count, dtype=jnp.int32)[:, None]
    slot_length = jnp.sum(jnp.where(placing, lengths[None, :], 0), axis=1)
    placing_matrix = placing.astype(jnp.bfloat16)
    slot_wave = jnp.dot(placing_matrix, waveform, preferred_element_type=jnp.float32).astype(
        jnp.bfloat16
    )
    got_wave, got_length = (
        lax.all_to_all(
            slot_wave.reshape(dp_size, slot_cap, -1), "dp", split_axis=0, concat_axis=0, tiled=True
        ),
        lax.all_to_all(
            slot_length.reshape(dp_size, slot_cap), "dp", split_axis=0, concat_axis=0, tiled=True
        ),
    )
    hidden = encode(
        got_wave.reshape(slot_count, -1), conv0_weight, conv1_weight, norm_gain, norm_bias
    )
    got_length = got_length.reshape(slot_count)
    normed = layer_norm(hidden.astype(jnp.float32), norm_gain[2], norm_bias[2]).astype(jnp.bfloat16)
    frame_ids = jnp.arange(frame_count, dtype=jnp.int32)
    valid = (10 * frame_ids[None, :] + 20 <= got_length[:, None]).reshape(-1, 1)
    frame_mask = valid.astype(jnp.float32)
    projected = jnp.dot(normed, weights, preferred_element_type=jnp.float32) + biases.astype(
        jnp.float32
    )
    features = (projected * frame_mask).astype(jnp.bfloat16).reshape(slot_count, frame_count, -1)
    cot_rows = cotangent.reshape(slot_count * frame_count, -1)
    grad_out = jnp.where(valid, cot_rows, jnp.zeros_like(cot_rows))
    weight_term = lax.dot_general(
        normed, grad_out, (((0,), (0,)), ((), ())), preferred_element_type=jnp.float32
    )
    bias_term = jnp.sum(grad_out, axis=0, dtype=jnp.float32)
    part_weight, part_bias = (
        lax.psum_scatter(weight_term, "fsdp", scatter_dimension=1, tiled=True),
        lax.psum_scatter(bias_term, "fsdp", scatter_dimension=0, tiled=True),
    )
    grad_weight, grad_bias = lax.psum((part_weight, part_bias), "dp")
    return (features, grad_weight.astype(jnp.bfloat16), grad_bias.astype(jnp.bfloat16))


def solution(mesh):
    in_specs = (
        P(("dp", "fsdp"), None),
        P(("dp", "fsdp"), None),
        P(("dp", "fsdp")),
        P(),
        P(),
        P(),
        P(),
        P(None, "fsdp"),
        P("fsdp"),
        P(("dp", "fsdp"), None, None),
    )
    out_specs = (P(("dp", "fsdp"), None, None), P(None, "fsdp"), P("fsdp"))
    body = local_fused if (mesh.shape["dp"], mesh.shape["fsdp"]) == (8, 4) else local
    return jax.shard_map(body, mesh=mesh, in_specs=in_specs, out_specs=out_specs, check_vma=False)
```

```python
import functools
import math

import jax
import jax.numpy as jnp
from jax import lax
from jax.experimental import pallas as pl
from jax.experimental.pallas import tpu as pltpu
from jax.sharding import PartitionSpec as P

MESH = pl.DeviceIdType.MESH
F32 = jnp.float32
BF16 = jnp.bfloat16


def gelu(v):
    return 0.5 * v * (1.0 + lax.erf(v * (1.0 / math.sqrt(2.0))))


def norm_rows(values, gain_vec, bias_vec):
    avg = jnp.mean(values, axis=-1, keepdims=True)
    centred = values - avg
    var = jnp.mean(centred * centred, axis=-1, keepdims=True)
    return centred * lax.rsqrt(var + 1e-05) * gain_vec + bias_vec


def dot_t(a, b):
    return lax.dot_general(a, b, (((0,), (0,)), ((), ())), preferred_element_type=F32)


def fused(
    samp, n_dp, n_f, cap, frames,
    wave_ref, dest_ref, len_ref, w0_ref, w1_hbm, gain_ref, nbias_ref, pw_hbm, pb_ref, cot_hbm,
    feat_hbm, gw_ref, gb_ref,
    w1_ref, pw_ref, cot_ref, feat_ref, l_sem, b2send, table_ref, xsend, xrecv, w0p, wfull, pbfull, cotb, normed_ref, masked_ref, mask_ref,
    asend, arecv, gown, bsend, brecv, csend, crecv, gwbuf,
    hsend, hrecv, hsum, hall,
    x_s, x_r, wz_s, wz_r, wp_s, wp_r, wm_s, wm_r, pb_s, pb_r,
    a_s, a_r, b_s, b_r, c_s, c_r, d_s, d_r, e_s, e_r, h_s, h_r, k_s, k_r,
):
    d = lax.axis_index("dp")
    f = lax.axis_index("fsdp")
    core = d % 2
    chip = d // 2
    cx = chip % 2
    cy = chip // 2
    n_chip = n_dp // 2
    cols, depth = pw_hbm.shape
    half = depth // 2
    ch = half // n_chip
    slots = n_dp * cap
    mate = chip * 2 + (1 - core)
    along_x = cy * 2 + (1 - cx)
    along_y = (1 - cy) * 2 + cx
    near = along_x * (1 - core) + along_y * core
    far = along_y * (1 - core) + along_x * core

    def other(c):
        return ((cy + c // 2) % 2) * 2 + (cx + c % 2) % 2

    def copy(src, dst, s_sem, r_sem, dd, ff):
        return pltpu.make_async_remote_copy(
            src_ref=src, dst_ref=dst, send_sem=s_sem, recv_sem=r_sem,
            device_id=(dd, ff), device_id_type=MESH,
        )

    pw_cp = pltpu.make_async_copy(pw_hbm, pw_ref, l_sem.at[0])
    cot_cp = pltpu.make_async_copy(cot_hbm, cot_ref, l_sem.at[1])
    w1_cp = pltpu.make_async_copy(w1_hbm, w1_ref, l_sem.at[2])
    for one in (pw_cp, cot_cp, w1_cp):
        one.start()
    barrier = pltpu.get_barrier_semaphore()
    for o in range(1, n_dp):
        pl.semaphore_signal(barrier, inc=1, device_id=((d + o) % n_dp, f), device_id_type=MESH)
    for o in range(1, n_f):
        pl.semaphore_signal(barrier, inc=1, device_id=(d, (f + o) % n_f), device_id_type=MESH)

    rows = wave_ref.shape[0]
    tri_r = lax.broadcasted_iota(jnp.int32, (rows, rows), 0)
    tri_c = lax.broadcasted_iota(jnp.int32, (rows, rows), 1)
    lane = lax.broadcasted_iota(jnp.int32, (rows, 128), 1)
    spread = jnp.broadcast_to(len_ref[...].astype(F32), (rows, rows))
    span = jnp.sum(jnp.where(tri_r == tri_c, spread, 0.0), axis=1, keepdims=True)
    table_ref[...] = jnp.where(lane == samp, span, 0.0).astype(BF16)
    table_ref[:, 0:samp] = wave_ref[...]
    table = table_ref[...]
    lane = lane.astype(F32)
    named_row = jnp.broadcast_to(dest_ref[...].astype(F32), (rows, rows))
    target = jnp.sum(jnp.where(tri_r == tri_c, named_row, 0.0), axis=1, keepdims=True)
    named = (target == lane).astype(F32)
    earlier = (tri_c < tri_r).astype(F32).astype(BF16)
    before = jnp.dot(earlier, named.astype(BF16), preferred_element_type=F32)
    rank = jnp.sum(before * named, axis=1, keepdims=True)
    place = target * cap + rank
    placing = (place == lane).astype(F32).astype(BF16)
    placed = dot_t(placing, table)[:slots]
    xsend[...] = placed.reshape(n_dp, cap, 128)
    eye_r = lax.broadcasted_iota(jnp.int32, (depth, depth), 0)
    eye_c = lax.broadcasted_iota(jnp.int32, (depth, depth), 1)
    eye = (eye_r == eye_c).astype(F32).astype(BF16)
    pw_cp.wait()
    wfull[f] = lax.dot_general(
        eye, pw_ref[...], (((1,), (1,)), ((), ())), preferred_element_type=F32).astype(BF16)
    pbfull[f] = jnp.broadcast_to(pb_ref[...].astype(F32)[None, :], (8, cols))
    pl.semaphore_wait(barrier, n_dp + n_f - 2)

    x_cp = []
    for o in range(1, n_dp):
        p = (d + o) % n_dp
        x_cp.append(copy(xsend.at[p], xrecv.at[d], x_s.at[o], x_r.at[o], p, f))
        x_cp[-1].start()
    mine = core * half + chip * ch
    z_cp, pb_cp = [], []
    for o in range(1, n_f):
        p = (f + o) % n_f
        z_cp.append(copy(
            wfull.at[f, pl.ds(mine, ch)], wfull.at[f, pl.ds(mine, ch)],
            wz_s.at[o], wz_r.at[o], d, p))
        z_cp[-1].start()
        pb_cp.append(copy(pbfull.at[f], pbfull.at[f], pb_s.at[o], pb_r.at[o], d, p))
        pb_cp[-1].start()
    xrecv[d] = xsend[d]
    w0p[...] = jnp.zeros_like(w0p)
    w0p[0 : w0_ref.shape[0], :] = w0_ref[...]
    cot_cp.wait()
    for b in range(n_f):
        cotb[b] = cot_ref[:, b * cols : (b + 1) * cols]
    for o in range(1, n_dp):
        q = (d + n_dp - o) % n_dp
        copy(xsend.at[q], xrecv.at[q], x_s.at[o], x_r.at[o], q, f).wait_recv()

    x = xrecv[...].reshape(slots, 128)
    length = x[:, samp : samp + 1]
    first, p_cp = [], []
    for t in range(2 * frames + 1):
        xt = x if t == 0 else pltpu.roll(x, 128 - 5 * t, axis=1)
        v = jnp.dot(xt.astype(BF16), w0p[...], preferred_element_type=F32)
        first.append(gelu(norm_rows(v, gain_ref[0:1], nbias_ref[0:1])).astype(BF16))
        for o in range(1, n_f):
            if t != (2 * frames + 1) * o // n_f:
                continue
            q = (f + n_f - o) % n_f
            part = wfull.at[q, pl.ds(mine, ch)]
            copy(part, part, wz_s.at[o], wz_r.at[o], d, q).wait_recv()
            for c in range(1, n_chip):
                i = o * n_chip + c
                p_cp.append(copy(part, part, wp_s.at[i], wp_r.at[i], other(c) * 2 + core, f))
                p_cp[-1].start()

    w1_cp.wait()
    normed, masked, masks = [], [], []
    for j in range(frames):
        taps = jnp.concatenate(first[2 * j : 2 * j + 3], axis=1)
        v = jnp.dot(taps, w1_ref[...], preferred_element_type=F32)
        hid = gelu(norm_rows(v, gain_ref[1:2], nbias_ref[1:2])).astype(BF16).astype(F32)
        nj = norm_rows(hid, gain_ref[2:3], nbias_ref[2:3]).astype(BF16)
        mj = (length >= 10.0 * j + 20.0).astype(F32)
        normed.append(nj)
        masks.append(jnp.broadcast_to(mj, (slots, 128)).astype(BF16))
    total = slots * frames
    pr = lax.broadcasted_iota(jnp.int32, (total, total), 0)
    pc = lax.broadcasted_iota(jnp.int32, (total, total), 1)
    perm = ((pr % frames) * slots + pr // frames == pc).astype(F32).astype(BF16)
    nrm = jnp.dot(perm, jnp.concatenate(normed, axis=0), preferred_element_type=F32)
    msk = jnp.dot(perm, jnp.concatenate(masks, axis=0), preferred_element_type=F32)
    normed_ref[...] = nrm.astype(BF16)
    masked_ref[...] = (nrm * msk[:, 0:1]).astype(BF16)
    mask_ref[...] = msk

    order = [o % n_f for o in range(1, n_f + 1)]
    a_cp = []
    theirs = masked_ref[:, pl.ds(pl.multiple_of((1 - core) * half, half), half)]
    for o in order:
        b = (f + o) % n_f
        asend[o] = dot_t(theirs, cotb[b]).astype(BF16)
        a_cp.append(copy(asend.at[o], arecv.at[o], a_s.at[o], a_r.at[o], mate, f))
        a_cp[-1].start()
    ours = masked_ref[:, pl.ds(pl.multiple_of(core * half, half), half)]
    for o in order:
        b = (f + o) % n_f
        gown[o] = dot_t(ours, cotb[b])
    h_cp = []
    ones = mask_ref[...].astype(BF16)
    for o in order:
        b = (f + o) % n_f
        hsend[o] = dot_t(ones, cotb[b])[0:8]
        if o:
            h_cp.append(copy(hsend.at[o], hrecv.at[o], h_s.at[o], h_r.at[o], d, b))
            h_cp[-1].start()

    b_cp = []
    for o in order:
        copy(asend.at[o], arecv.at[o], a_s.at[o], a_r.at[o], mate, f).wait_recv()
        both = gown[o] + arecv[o].astype(F32)
        gown[o] = both
        bsend[o] = both.astype(BF16)
        for c, to in ((2, 3 - chip), (1, near)):
            i = o * n_chip + c
            b_cp.append(copy(
                bsend.at[o, pl.ds(to * ch, ch)], brecv.at[i],
                b_s.at[i], b_r.at[i], near * 2 + core, f))
            b_cp[-1].start()

    m_cp = []
    for o in range(1, n_f):
        q = (f + n_f - o) % n_f
        for c in range(1, n_chip):
            i = o * n_chip + c
            theirs_at = core * half + other(c) * ch
            part = wfull.at[q, pl.ds(theirs_at, ch)]
            copy(part, part, wp_s.at[i], wp_r.at[i], other(c) * 2 + core, f).wait_recv()
        block = wfull.at[q, pl.ds(core * half, half)]
        m_cp.append(copy(block, block, wm_s.at[o], wm_r.at[o], mate, f))
        m_cp[-1].start()
        copy(pbfull.at[q], pbfull.at[q], pb_s.at[o], pb_r.at[o], d, q).wait_recv()
    for o in order:
        i = o * n_chip
        copy(brecv.at[i + 2], brecv.at[i + 2], b_s.at[i + 2], b_r.at[i + 2], near * 2 + core, f).wait_recv()
        b2send[o] = (gown[o, pl.ds(far * ch, ch), :] + brecv[i + 2].astype(F32)).astype(BF16)
        b_cp.append(copy(
            b2send.at[o], brecv.at[i + 3], b_s.at[i + 3], b_r.at[i + 3], far * 2 + core, f))
        b_cp[-1].start()
    for o in range(1, n_f):
        q = (f + n_f - o) % n_f
        block = wfull.at[q, pl.ds((1 - core) * half, half)]
        copy(block, block, wm_s.at[o], wm_r.at[o], mate, f).wait_recv()
    def project(b):
        v = jnp.dot(normed_ref[...], wfull[b], preferred_element_type=F32) + pbfull[b][0:1]
        feat_ref[:, b * cols : (b + 1) * cols] = (v * mask_ref[:, 0:1]).astype(BF16)

    for b in range(n_f // 2):
        project(b)

    c_cp = []
    own = None
    for o in order:
        part = gown[o, pl.ds(chip * ch, ch), :]
        for c, to in ((1, near), (3, far)):
            i = o * n_chip + c
            copy(brecv.at[i], brecv.at[i], b_s.at[i], b_r.at[i], to * 2 + core, f).wait_recv()
            part = part + brecv[i].astype(F32)
        if o:
            csend[o] = part.astype(BF16)
            c_cp.append(copy(csend.at[o], crecv.at[o], c_s.at[o], c_r.at[o], d, (f + o) % n_f))
            c_cp[-1].start()
        else:
            own = part
    for b in range(n_f // 2, n_f):
        project(b)
    feat_cp = pltpu.make_async_copy(feat_ref, feat_hbm, l_sem.at[3])
    feat_cp.start()
    hown = hsend[0]
    for o in range(1, n_f):
        q = (f + n_f - o) % n_f
        copy(hsend.at[o], hrecv.at[o], h_s.at[o], h_r.at[o], d, q).wait_recv()
        hown = hown + hrecv[o]
    hsum[...] = hown
    k_cp = []
    for o in range(1, n_dp):
        k_cp.append(copy(hsum, hall.at[o], k_s.at[o], k_r.at[o], (d + o) % n_dp, f))
        k_cp[-1].start()
    for o in range(1, n_f):
        q = (f + n_f - o) % n_f
        copy(csend.at[o], crecv.at[o], c_s.at[o], c_r.at[o], d, q).wait_recv()
        own = own + crecv[o].astype(F32)
    gwbuf[pl.ds(mine, ch), :] = own.astype(BF16)

    d_cp = []
    src = gwbuf.at[pl.ds(mine, ch)]
    for c in range(1, n_chip):
        d_cp.append(copy(src, src, d_s.at[c], d_r.at[c], other(c) * 2 + core, f))
        d_cp[-1].start()
    e_cp = [copy(src, src, e_s.at[0], e_r.at[0], mate, f)]
    e_cp[0].start()
    for c in range(1, n_chip):
        part = gwbuf.at[pl.ds(core * half + other(c) * ch, ch)]
        copy(part, part, d_s.at[c], d_r.at[c], other(c) * 2 + core, f).wait_recv()
        e_cp.append(copy(part, part, e_s.at[c], e_r.at[c], mate, f))
        e_cp[-1].start()
    for o in range(1, n_dp):
        copy(hsum, hall.at[o], k_s.at[o], k_r.at[o], (d + n_dp - o) % n_dp, f).wait_recv()
        hown = hown + hall[o]
    gb_ref[...] = hown[0].astype(BF16)
    for c in range(n_chip):
        at = other(c) if c else chip
        part = gwbuf.at[pl.ds((1 - core) * half + at * ch, ch)]
        copy(part, part, e_s.at[c], e_r.at[c], mate, f).wait_recv()
    gw_ref[...] = dot_t(gwbuf[...], eye).astype(BF16)
    feat_cp.wait()
    for one in x_cp + z_cp + pb_cp + p_cp + m_cp + a_cp + h_cp + b_cp + c_cp + k_cp + d_cp + e_cp:
        one.wait_send()


def local_fused(
    waveform, destination, lengths, conv0_weight, conv1_weight,
    norm_gain, norm_bias, proj_weight, proj_bias, cotangent,
):
    n_dp, n_f = lax.axis_size("dp"), lax.axis_size("fsdp")
    rows, samp = waveform.shape
    slots, frames, width = cotangent.shape
    cap = slots // n_dp
    depth, cols = proj_weight.shape
    n_chip, half = n_dp // 2, depth // 2
    ch = half // n_chip
    total = slots * frames
    vmem = pl.BlockSpec(memory_space=pltpu.VMEM)
    hbm = pl.BlockSpec(memory_space=pltpu.HBM)
    dma = lambda n: pltpu.SemaphoreType.DMA((n,))
    nc = n_f * n_chip
    feats, gw, gb = pl.pallas_call(
        functools.partial(fused, samp, n_dp, n_f, cap, frames),
        out_shape=(
            jax.ShapeDtypeStruct((total, width), BF16),
            jax.ShapeDtypeStruct((cols, depth), BF16),
            jax.ShapeDtypeStruct((cols,), BF16),
        ),
        in_specs=[vmem] * 4 + [hbm] + [vmem] * 2 + [hbm, vmem, hbm],
        out_specs=(hbm, vmem, vmem),
        scratch_shapes=[
            pltpu.VMEM(conv1_weight.shape, BF16),
            pltpu.VMEM((cols, depth), BF16),
            pltpu.VMEM((total, width), BF16),
            pltpu.VMEM((total, width), BF16),
            dma(4),
            pltpu.VMEM((n_f, ch, cols), BF16),
            pltpu.VMEM((rows, 128), BF16),
            pltpu.VMEM((n_dp, cap, 128), F32),
            pltpu.VMEM((n_dp, cap, 128), F32),
            pltpu.VMEM((128, depth), BF16),
            pltpu.VMEM((n_f, depth, cols), BF16),
            pltpu.VMEM((n_f, 8, cols), F32),
            pltpu.VMEM((n_f, total, cols), BF16),
            pltpu.VMEM((total, depth), BF16),
            pltpu.VMEM((total, depth), BF16),
            pltpu.VMEM((total, 128), F32),
            pltpu.VMEM((n_f, half, cols), BF16),
            pltpu.VMEM((n_f, half, cols), BF16),
            pltpu.VMEM((n_f, half, cols), F32),
            pltpu.VMEM((n_f, half, cols), BF16),
            pltpu.VMEM((nc, ch, cols), BF16),
            pltpu.VMEM((n_f, ch, cols), BF16),
            pltpu.VMEM((n_f, ch, cols), BF16),
            pltpu.VMEM((depth, cols), BF16),
            pltpu.VMEM((n_f, 8, cols), F32),
            pltpu.VMEM((n_f, 8, cols), F32),
            pltpu.VMEM((8, cols), F32),
            pltpu.VMEM((n_dp, 8, cols), F32),
            dma(n_dp), dma(n_dp), dma(n_f), dma(n_f), dma(nc), dma(nc),
            dma(n_f), dma(n_f), dma(n_f), dma(n_f),
            dma(n_f), dma(n_f), dma(nc), dma(nc), dma(n_f), dma(n_f),
            dma(n_chip), dma(n_chip), dma(n_chip), dma(n_chip),
            dma(n_f), dma(n_f), dma(n_dp), dma(n_dp),
        ],
        compiler_params=pltpu.CompilerParams(
            collective_id=0, has_side_effects=True, vmem_limit_bytes=60 * 1024 * 1024),
        cost_estimate=pl.CostEstimate(
            flops=2 * total * depth * (3 * depth + 2 * width),
            bytes_accessed=8 * depth * width, transcendentals=13 * slots * depth),
    )(waveform, destination.reshape(1, -1), lengths[None, :], conv0_weight, conv1_weight,
      norm_gain, norm_bias, proj_weight.T, proj_bias, cotangent.reshape(total, width))
    return feats.reshape(slots, frames, width), gw.T, gb


def layer_norm(values, gain_vec, bias_vec):
    avg_value = jnp.mean(values, axis=-1, keepdims=True)
    centred = values - avg_value
    variance = jnp.mean(centred * centred, axis=-1, keepdims=True)
    return centred * lax.rsqrt(variance + 1e-05) * gain_vec + bias_vec


def encode(wave_rows, conv0_weight, conv1_weight, norm_gain, norm_bias):
    row_count = wave_rows.shape[0]
    frame_count = (wave_rows.shape[1] - 10) // 10
    sample_blocks = wave_rows.reshape(row_count, 2 * frame_count + 2, 5)
    sample_pairs = jnp.concatenate([sample_blocks[:, :-1], sample_blocks[:, 1:]], axis=2).reshape(
        -1, 10
    )
    first_conv = jnp.dot(sample_pairs, conv0_weight, preferred_element_type=jnp.float32)
    first_conv = jax.nn.gelu(
        layer_norm(first_conv, norm_gain[0], norm_bias[0]), approximate=False
    ).astype(jnp.bfloat16)
    first_conv = first_conv.reshape(row_count, 2 * frame_count + 1, -1)
    conv_taps = jnp.concatenate(
        [
            first_conv[:, 0 : 2 * frame_count : 2],
            first_conv[:, 1 : 2 * frame_count + 1 : 2],
            first_conv[:, 2 : 2 * frame_count + 2 : 2],
        ],
        axis=2,
    )
    second_conv = jnp.dot(
        conv_taps.reshape(row_count * frame_count, -1),
        conv1_weight,
        preferred_element_type=jnp.float32,
    )
    return jax.nn.gelu(
        layer_norm(second_conv, norm_gain[1], norm_bias[1]), approximate=False
    ).astype(jnp.bfloat16)


def local(
    waveform,
    destination,
    lengths,
    conv0_weight,
    conv1_weight,
    norm_gain,
    norm_bias,
    proj_weight,
    proj_bias,
    cotangent,
):
    dp_size = lax.axis_size("dp")
    row_count = waveform.shape[0]
    slot_count = cotangent.shape[0]
    frame_count = cotangent.shape[1]
    slot_cap = slot_count // dp_size
    weights, biases = (
        lax.all_gather(proj_weight, "fsdp", axis=1, tiled=True),
        lax.all_gather(proj_bias, "fsdp", axis=0, tiled=True),
    )
    targets = destination[:, 0]
    row_order = jnp.arange(row_count, dtype=jnp.int32)
    same_dest = targets[:, None] == targets[None, :]
    earlier_rows = row_order[None, :] < row_order[:, None]
    row_rank = jnp.sum((same_dest & earlier_rows).astype(jnp.int32), axis=1)
    position = targets * slot_cap + row_rank
    placing = position[None, :] == jnp.arange(slot_count, dtype=jnp.int32)[:, None]
    slot_length = jnp.sum(jnp.where(placing, lengths[None, :], 0), axis=1)
    placing_matrix = placing.astype(jnp.bfloat16)
    slot_wave = jnp.dot(placing_matrix, waveform, preferred_element_type=jnp.float32).astype(
        jnp.bfloat16
    )
    got_wave, got_length = (
        lax.all_to_all(
            slot_wave.reshape(dp_size, slot_cap, -1), "dp", split_axis=0, concat_axis=0, tiled=True
        ),
        lax.all_to_all(
            slot_length.reshape(dp_size, slot_cap), "dp", split_axis=0, concat_axis=0, tiled=True
        ),
    )
    hidden = encode(
        got_wave.reshape(slot_count, -1), conv0_weight, conv1_weight, norm_gain, norm_bias
    )
    got_length = got_length.reshape(slot_count)
    normed = layer_norm(hidden.astype(jnp.float32), norm_gain[2], norm_bias[2]).astype(jnp.bfloat16)
    frame_ids = jnp.arange(frame_count, dtype=jnp.int32)
    valid = (10 * frame_ids[None, :] + 20 <= got_length[:, None]).reshape(-1, 1)
    frame_mask = valid.astype(jnp.float32)
    projected = jnp.dot(normed, weights, preferred_element_type=jnp.float32) + biases.astype(
        jnp.float32
    )
    features = (projected * frame_mask).astype(jnp.bfloat16).reshape(slot_count, frame_count, -1)
    cot_rows = cotangent.reshape(slot_count * frame_count, -1)
    grad_out = jnp.where(valid, cot_rows, jnp.zeros_like(cot_rows))
    weight_term = lax.dot_general(
        normed, grad_out, (((0,), (0,)), ((), ())), preferred_element_type=jnp.float32
    )
    bias_term = jnp.sum(grad_out, axis=0, dtype=jnp.float32)
    part_weight, part_bias = (
        lax.psum_scatter(weight_term, "fsdp", scatter_dimension=1, tiled=True),
        lax.psum_scatter(bias_term, "fsdp", scatter_dimension=0, tiled=True),
    )
    grad_weight, grad_bias = lax.psum((part_weight, part_bias), "dp")
    return (features, grad_weight.astype(jnp.bfloat16), grad_bias.astype(jnp.bfloat16))


def solution(mesh):
    in_specs = (
        P(("dp", "fsdp"), None),
        P(("dp", "fsdp"), None),
        P(("dp", "fsdp")),
        P(),
        P(),
        P(),
        P(),
        P(None, "fsdp"),
        P("fsdp"),
        P(("dp", "fsdp"), None, None),
    )
    out_specs = (P(("dp", "fsdp"), None, None), P(None, "fsdp"), P("fsdp"))
    body = local_fused if (mesh.shape["dp"], mesh.shape["fsdp"]) == (8, 4) else local
    return jax.shard_map(body, mesh=mesh, in_specs=in_specs, out_specs=out_specs, check_vma=False)
```

```python
import functools
import math

import jax
import jax.numpy as jnp
from jax import lax
from jax.experimental import pallas as pl
from jax.experimental.pallas import tpu as pltpu
from jax.sharding import PartitionSpec as P

MESH = pl.DeviceIdType.MESH
F32 = jnp.float32
BF16 = jnp.bfloat16


def gelu(v):
    return 0.5 * v * (1.0 + lax.erf(v * (1.0 / math.sqrt(2.0))))


def norm_rows(values, gain_vec, bias_vec):
    avg = jnp.mean(values, axis=-1, keepdims=True)
    centred = values - avg
    var = jnp.mean(centred * centred, axis=-1, keepdims=True)
    return centred * lax.rsqrt(var + 1e-05) * gain_vec + bias_vec


def dot_t(a, b):
    return lax.dot_general(a, b, (((0,), (0,)), ((), ())), preferred_element_type=F32)


def fused(
    samp, n_dp, n_f, cap, frames,
    wave_ref, dest_ref, len_ref, w0_ref, w1_hbm, gain_ref, nbias_ref, pw_ref, pb_ref, cot_ref,
    feat_ref, gw_ref, gb_ref,
    w1_ref, w1_sem, perm_ref, table_ref, xsend, xrecv, w0p, wfull, pbfull, cotb, normed_ref, masked_ref, mask_ref,
    asend, arecv, gown, bsend, brecv, csend, crecv, gwbuf,
    hsend, hrecv, hsum, hall,
    x_s, x_r, wz_s, wz_r, wp_s, wp_r, wm_s, wm_r, pb_s, pb_r,
    a_s, a_r, b_s, b_r, c_s, c_r, d_s, d_r, e_s, e_r, h_s, h_r, k_s, k_r,
):
    d = lax.axis_index("dp")
    f = lax.axis_index("fsdp")
    core = d % 2
    chip = d // 2
    cx = chip % 2
    cy = chip // 2
    n_chip = n_dp // 2
    cols, depth = pw_ref.shape
    half = depth // 2
    ch = half // n_chip
    slots = n_dp * cap
    mate = chip * 2 + (1 - core)

    def other(c):
        return ((cy + c // 2) % 2) * 2 + (cx + c % 2) % 2

    def copy(src, dst, s_sem, r_sem, dd, ff):
        return pltpu.make_async_remote_copy(
            src_ref=src, dst_ref=dst, send_sem=s_sem, recv_sem=r_sem,
            device_id=(dd, ff), device_id_type=MESH,
        )

    w1_cp = pltpu.make_async_copy(w1_hbm, w1_ref, w1_sem)
    w1_cp.start()
    barrier = pltpu.get_barrier_semaphore()
    for o in range(1, n_dp):
        pl.semaphore_signal(barrier, inc=1, device_id=((d + o) % n_dp, f), device_id_type=MESH)
    for o in range(1, n_f):
        pl.semaphore_signal(barrier, inc=1, device_id=(d, (f + o) % n_f), device_id_type=MESH)

    rows = wave_ref.shape[0]
    tri_r = lax.broadcasted_iota(jnp.int32, (rows, rows), 0)
    tri_c = lax.broadcasted_iota(jnp.int32, (rows, rows), 1)
    lane = lax.broadcasted_iota(jnp.int32, (rows, 128), 1)
    spread = jnp.broadcast_to(len_ref[...].astype(F32), (rows, rows))
    span = jnp.sum(jnp.where(tri_r == tri_c, spread, 0.0), axis=1, keepdims=True)
    table_ref[...] = jnp.where(lane == samp, span, 0.0).astype(BF16)
    table_ref[:, 0:samp] = wave_ref[...]
    table = table_ref[...]
    lane = lane.astype(F32)
    named_row = jnp.broadcast_to(dest_ref[...].astype(F32), (rows, rows))
    target = jnp.sum(jnp.where(tri_r == tri_c, named_row, 0.0), axis=1, keepdims=True)
    named = (target == lane).astype(F32)
    earlier = (tri_c < tri_r).astype(F32).astype(BF16)
    before = jnp.dot(earlier, named.astype(BF16), preferred_element_type=F32)
    rank = jnp.sum(before * named, axis=1, keepdims=True)
    place = target * cap + rank
    placing = (place == lane).astype(F32).astype(BF16)
    placed = dot_t(placing, table)[:slots]
    xsend[...] = placed.reshape(n_dp, cap, 128)
    pl.semaphore_wait(barrier, n_dp + n_f - 2)

    x_cp = []
    for o in range(1, n_dp):
        p = (d + o) % n_dp
        x_cp.append(copy(xsend.at[p], xrecv.at[d], x_s.at[o], x_r.at[o], p, f))
        x_cp[-1].start()
    eye_r = lax.broadcasted_iota(jnp.int32, (depth, depth), 0)
    eye_c = lax.broadcasted_iota(jnp.int32, (depth, depth), 1)
    eye = (eye_r == eye_c).astype(F32).astype(BF16)
    wfull[f] = lax.dot_general(
        eye, pw_ref[...], (((1,), (1,)), ((), ())), preferred_element_type=F32).astype(BF16)
    pbfull[f] = jnp.broadcast_to(pb_ref[...].astype(F32)[None, :], (8, cols))
    mine = core * half + chip * ch
    z_cp, pb_cp = [], []
    for o in range(1, n_f):
        p = (f + o) % n_f
        z_cp.append(copy(
            wfull.at[f, pl.ds(mine, ch)], wfull.at[f, pl.ds(mine, ch)],
            wz_s.at[o], wz_r.at[o], d, p))
        z_cp[-1].start()
        pb_cp.append(copy(pbfull.at[f], pbfull.at[f], pb_s.at[o], pb_r.at[o], d, p))
        pb_cp[-1].start()
    xrecv[d] = xsend[d]
    w0p[...] = jnp.zeros_like(w0p)
    w0p[0 : w0_ref.shape[0], :] = w0_ref[...]
    total = slots * frames
    pr = lax.broadcasted_iota(jnp.int32, (total, total), 0)
    pc = lax.broadcasted_iota(jnp.int32, (total, total), 1) * frames
    hit = pr == pc
    for j in range(1, frames):
        hit = hit | (pr == pc - j * (total - 1))
    perm_ref[...] = hit.astype(F32).astype(BF16)
    for b in range(n_f):
        cotb[b] = cot_ref[:, b * cols : (b + 1) * cols]
    for o in range(1, n_dp):
        q = (d + n_dp - o) % n_dp
        copy(xsend.at[q], xrecv.at[q], x_s.at[o], x_r.at[o], q, f).wait_recv()

    x = xrecv[...].reshape(slots, 128)
    length = x[:, samp : samp + 1]
    first, p_cp = [], []
    for t in range(2 * frames + 1):
        xt = x if t == 0 else pltpu.roll(x, 128 - 5 * t, axis=1)
        v = jnp.dot(xt.astype(BF16), w0p[...], preferred_element_type=F32)
        first.append(gelu(norm_rows(v, gain_ref[0:1], nbias_ref[0:1])).astype(BF16))
        for o in range(1, n_f):
            if t != (2 * frames + 1) * o // n_f:
                continue
            q = (f + n_f - o) % n_f
            part = wfull.at[q, pl.ds(mine, ch)]
            copy(part, part, wz_s.at[o], wz_r.at[o], d, q).wait_recv()
            for c in range(1, n_chip):
                i = o * n_chip + c
                p_cp.append(copy(part, part, wp_s.at[i], wp_r.at[i], other(c) * 2 + core, f))
                p_cp[-1].start()

    w1_cp.wait()
    normed, masked, masks = [], [], []
    for j in range(frames):
        taps = jnp.concatenate(first[2 * j : 2 * j + 3], axis=1)
        v = jnp.dot(taps, w1_ref[...], preferred_element_type=F32)
        hid = gelu(norm_rows(v, gain_ref[1:2], nbias_ref[1:2])).astype(BF16).astype(F32)
        nj = norm_rows(hid, gain_ref[2:3], nbias_ref[2:3]).astype(BF16)
        mj = (length >= 10.0 * j + 20.0).astype(F32)
        normed.append(nj)
        masks.append(jnp.broadcast_to(mj, (slots, 128)).astype(BF16))
    nrm = jnp.dot(perm_ref[...], jnp.concatenate(normed, axis=0), preferred_element_type=F32)
    msk = jnp.dot(perm_ref[...], jnp.concatenate(masks, axis=0), preferred_element_type=F32)
    normed_ref[...] = nrm.astype(BF16)
    masked_ref[...] = (nrm * msk[:, 0:1]).astype(BF16)
    mask_ref[...] = msk

    order = [o % n_f for o in range(1, n_f + 1)]
    a_cp = []
    theirs = masked_ref[:, pl.ds(pl.multiple_of((1 - core) * half, half), half)]
    for o in order:
        b = (f + o) % n_f
        asend[o] = dot_t(theirs, cotb[b]).astype(BF16)
        a_cp.append(copy(asend.at[o], arecv.at[o], a_s.at[o], a_r.at[o], mate, f))
        a_cp[-1].start()
    ours = masked_ref[:, pl.ds(pl.multiple_of(core * half, half), half)]
    for o in order:
        b = (f + o) % n_f
        gown[o] = dot_t(ours, cotb[b])
    b_cp = []
    for o in order:
        copy(asend.at[o], arecv.at[o], a_s.at[o], a_r.at[o], mate, f).wait_recv()
        both = gown[o] + arecv[o].astype(F32)
        gown[o] = both
        bsend[o] = both.astype(BF16)
        for c in range(1, n_chip):
            to = other(c)
            i = o * n_chip + c
            b_cp.append(copy(
                bsend.at[o, pl.ds(to * ch, ch)], brecv.at[i],
                b_s.at[i], b_r.at[i], to * 2 + core, f))
            b_cp[-1].start()

    h_cp = []
    ones = mask_ref[...].astype(BF16)
    for o in order:
        b = (f + o) % n_f
        hsend[o] = dot_t(ones, cotb[b])[0:8]
        if o:
            h_cp.append(copy(hsend.at[o], hrecv.at[o], h_s.at[o], h_r.at[o], d, b))
            h_cp[-1].start()

    m_cp = []
    for o in range(1, n_f):
        q = (f + n_f - o) % n_f
        for c in range(1, n_chip):
            i = o * n_chip + c
            theirs_at = core * half + other(c) * ch
            part = wfull.at[q, pl.ds(theirs_at, ch)]
            copy(part, part, wp_s.at[i], wp_r.at[i], other(c) * 2 + core, f).wait_recv()
        block = wfull.at[q, pl.ds(core * half, half)]
        m_cp.append(copy(block, block, wm_s.at[o], wm_r.at[o], mate, f))
        m_cp[-1].start()
        copy(pbfull.at[q], pbfull.at[q], pb_s.at[o], pb_r.at[o], d, q).wait_recv()
    for o in range(1, n_f):
        q = (f + n_f - o) % n_f
        block = wfull.at[q, pl.ds((1 - core) * half, half)]
        copy(block, block, wm_s.at[o], wm_r.at[o], mate, f).wait_recv()
    def project(b):
        v = jnp.dot(normed_ref[...], wfull[b], preferred_element_type=F32) + pbfull[b][0:1]
        feat_ref[:, b * cols : (b + 1) * cols] = (v * mask_ref[:, 0:1]).astype(BF16)

    for b in range(n_f // 2):
        project(b)

    c_cp = []
    own = None
    for o in order:
        part = gown[o, pl.ds(chip * ch, ch), :]
        for c in range(1, n_chip):
            i = o * n_chip + c
            copy(brecv.at[i], brecv.at[i], b_s.at[i], b_r.at[i], other(c) * 2 + core, f).wait_recv()
            part = part + brecv[i].astype(F32)
        if o:
            csend[o] = part.astype(BF16)
            c_cp.append(copy(csend.at[o], crecv.at[o], c_s.at[o], c_r.at[o], d, (f + o) % n_f))
            c_cp[-1].start()
        else:
            own = part
    for b in range(n_f // 2, n_f):
        project(b)
    hown = hsend[0]
    for o in range(1, n_f):
        q = (f + n_f - o) % n_f
        copy(hsend.at[o], hrecv.at[o], h_s.at[o], h_r.at[o], d, q).wait_recv()
        hown = hown + hrecv[o]
    hsum[...] = hown
    k_cp = []
    for o in range(1, n_dp):
        k_cp.append(copy(hsum, hall.at[o], k_s.at[o], k_r.at[o], (d + o) % n_dp, f))
        k_cp[-1].start()
    for o in range(1, n_f):
        q = (f + n_f - o) % n_f
        copy(csend.at[o], crecv.at[o], c_s.at[o], c_r.at[o], d, q).wait_recv()
        own = own + crecv[o].astype(F32)
    gwbuf[pl.ds(mine, ch), :] = own.astype(BF16)

    d_cp = []
    src = gwbuf.at[pl.ds(mine, ch)]
    for c in range(1, n_chip):
        d_cp.append(copy(src, src, d_s.at[c], d_r.at[c], other(c) * 2 + core, f))
        d_cp[-1].start()
    e_cp = [copy(src, src, e_s.at[0], e_r.at[0], mate, f)]
    e_cp[0].start()
    for c in range(1, n_chip):
        part = gwbuf.at[pl.ds(core * half + other(c) * ch, ch)]
        copy(part, part, d_s.at[c], d_r.at[c], other(c) * 2 + core, f).wait_recv()
        e_cp.append(copy(part, part, e_s.at[c], e_r.at[c], mate, f))
        e_cp[-1].start()
    for o in range(1, n_dp):
        copy(hsum, hall.at[o], k_s.at[o], k_r.at[o], (d + n_dp - o) % n_dp, f).wait_recv()
        hown = hown + hall[o]
    gb_ref[...] = hown[0].astype(BF16)
    for c in range(n_chip):
        at = other(c) if c else chip
        part = gwbuf.at[pl.ds((1 - core) * half + at * ch, ch)]
        copy(part, part, e_s.at[c], e_r.at[c], mate, f).wait_recv()
    gw_ref[...] = dot_t(gwbuf[...], eye).astype(BF16)
    for one in x_cp + z_cp + pb_cp + p_cp + m_cp + a_cp + h_cp + b_cp + c_cp + k_cp + d_cp + e_cp:
        one.wait_send()


def local_fused(
    waveform, destination, lengths, conv0_weight, conv1_weight,
    norm_gain, norm_bias, proj_weight, proj_bias, cotangent,
):
    n_dp, n_f = lax.axis_size("dp"), lax.axis_size("fsdp")
    rows, samp = waveform.shape
    slots, frames, width = cotangent.shape
    cap = slots // n_dp
    depth, cols = proj_weight.shape
    n_chip, half = n_dp // 2, depth // 2
    ch = half // n_chip
    total = slots * frames
    vmem = pl.BlockSpec(memory_space=pltpu.VMEM)
    hbm = pl.BlockSpec(memory_space=pltpu.HBM)
    dma = lambda n: pltpu.SemaphoreType.DMA((n,))
    nc = n_f * n_chip
    feats, gw, gb = pl.pallas_call(
        functools.partial(fused, samp, n_dp, n_f, cap, frames),
        out_shape=(
            jax.ShapeDtypeStruct((total, width), BF16),
            jax.ShapeDtypeStruct((cols, depth), BF16),
            jax.ShapeDtypeStruct((cols,), BF16),
        ),
        in_specs=[vmem] * 4 + [hbm] + [vmem] * 5,
        out_specs=(vmem,) * 3,
        scratch_shapes=[
            pltpu.VMEM(conv1_weight.shape, BF16),
            pltpu.SemaphoreType.DMA,
            pltpu.VMEM((total, total), BF16),
            pltpu.VMEM((rows, 128), BF16),
            pltpu.VMEM((n_dp, cap, 128), F32),
            pltpu.VMEM((n_dp, cap, 128), F32),
            pltpu.VMEM((128, depth), BF16),
            pltpu.VMEM((n_f, depth, cols), BF16),
            pltpu.VMEM((n_f, 8, cols), F32),
            pltpu.VMEM((n_f, total, cols), BF16),
            pltpu.VMEM((total, depth), BF16),
            pltpu.VMEM((total, depth), BF16),
            pltpu.VMEM((total, 128), F32),
            pltpu.VMEM((n_f, half, cols), BF16),
            pltpu.VMEM((n_f, half, cols), BF16),
            pltpu.VMEM((n_f, half, cols), F32),
            pltpu.VMEM((n_f, half, cols), BF16),
            pltpu.VMEM((nc, ch, cols), BF16),
            pltpu.VMEM((n_f, ch, cols), BF16),
            pltpu.VMEM((n_f, ch, cols), BF16),
            pltpu.VMEM((depth, cols), BF16),
            pltpu.VMEM((n_f, 8, cols), F32),
            pltpu.VMEM((n_f, 8, cols), F32),
            pltpu.VMEM((8, cols), F32),
            pltpu.VMEM((n_dp, 8, cols), F32),
            dma(n_dp), dma(n_dp), dma(n_f), dma(n_f), dma(nc), dma(nc),
            dma(n_f), dma(n_f), dma(n_f), dma(n_f),
            dma(n_f), dma(n_f), dma(nc), dma(nc), dma(n_f), dma(n_f),
            dma(n_chip), dma(n_chip), dma(n_chip), dma(n_chip),
            dma(n_f), dma(n_f), dma(n_dp), dma(n_dp),
        ],
        compiler_params=pltpu.CompilerParams(
            collective_id=0, has_side_effects=True, vmem_limit_bytes=48 * 1024 * 1024),
        cost_estimate=pl.CostEstimate(
            flops=2 * total * depth * (3 * depth + 2 * width),
            bytes_accessed=8 * depth * width, transcendentals=13 * slots * depth),
    )(waveform, destination.reshape(1, -1), lengths[None, :], conv0_weight, conv1_weight,
      norm_gain, norm_bias, proj_weight.T, proj_bias, cotangent.reshape(total, width))
    return feats.reshape(slots, frames, width), gw.T, gb


def layer_norm(values, gain_vec, bias_vec):
    avg_value = jnp.mean(values, axis=-1, keepdims=True)
    centred = values - avg_value
    variance = jnp.mean(centred * centred, axis=-1, keepdims=True)
    return centred * lax.rsqrt(variance + 1e-05) * gain_vec + bias_vec


def encode(wave_rows, conv0_weight, conv1_weight, norm_gain, norm_bias):
    row_count = wave_rows.shape[0]
    frame_count = (wave_rows.shape[1] - 10) // 10
    sample_blocks = wave_rows.reshape(row_count, 2 * frame_count + 2, 5)
    sample_pairs = jnp.concatenate([sample_blocks[:, :-1], sample_blocks[:, 1:]], axis=2).reshape(
        -1, 10
    )
    first_conv = jnp.dot(sample_pairs, conv0_weight, preferred_element_type=jnp.float32)
    first_conv = jax.nn.gelu(
        layer_norm(first_conv, norm_gain[0], norm_bias[0]), approximate=False
    ).astype(jnp.bfloat16)
    first_conv = first_conv.reshape(row_count, 2 * frame_count + 1, -1)
    conv_taps = jnp.concatenate(
        [
            first_conv[:, 0 : 2 * frame_count : 2],
            first_conv[:, 1 : 2 * frame_count + 1 : 2],
            first_conv[:, 2 : 2 * frame_count + 2 : 2],
        ],
        axis=2,
    )
    second_conv = jnp.dot(
        conv_taps.reshape(row_count * frame_count, -1),
        conv1_weight,
        preferred_element_type=jnp.float32,
    )
    return jax.nn.gelu(
        layer_norm(second_conv, norm_gain[1], norm_bias[1]), approximate=False
    ).astype(jnp.bfloat16)


def local(
    waveform,
    destination,
    lengths,
    conv0_weight,
    conv1_weight,
    norm_gain,
    norm_bias,
    proj_weight,
    proj_bias,
    cotangent,
):
    dp_size = lax.axis_size("dp")
    row_count = waveform.shape[0]
    slot_count = cotangent.shape[0]
    frame_count = cotangent.shape[1]
    slot_cap = slot_count // dp_size
    weights, biases = (
        lax.all_gather(proj_weight, "fsdp", axis=1, tiled=True),
        lax.all_gather(proj_bias, "fsdp", axis=0, tiled=True),
    )
    targets = destination[:, 0]
    row_order = jnp.arange(row_count, dtype=jnp.int32)
    same_dest = targets[:, None] == targets[None, :]
    earlier_rows = row_order[None, :] < row_order[:, None]
    row_rank = jnp.sum((same_dest & earlier_rows).astype(jnp.int32), axis=1)
    position = targets * slot_cap + row_rank
    placing = position[None, :] == jnp.arange(slot_count, dtype=jnp.int32)[:, None]
    slot_length = jnp.sum(jnp.where(placing, lengths[None, :], 0), axis=1)
    placing_matrix = placing.astype(jnp.bfloat16)
    slot_wave = jnp.dot(placing_matrix, waveform, preferred_element_type=jnp.float32).astype(
        jnp.bfloat16
    )
    got_wave, got_length = (
        lax.all_to_all(
            slot_wave.reshape(dp_size, slot_cap, -1), "dp", split_axis=0, concat_axis=0, tiled=True
        ),
        lax.all_to_all(
            slot_length.reshape(dp_size, slot_cap), "dp", split_axis=0, concat_axis=0, tiled=True
        ),
    )
    hidden = encode(
        got_wave.reshape(slot_count, -1), conv0_weight, conv1_weight, norm_gain, norm_bias
    )
    got_length = got_length.reshape(slot_count)
    normed = layer_norm(hidden.astype(jnp.float32), norm_gain[2], norm_bias[2]).astype(jnp.bfloat16)
    frame_ids = jnp.arange(frame_count, dtype=jnp.int32)
    valid = (10 * frame_ids[None, :] + 20 <= got_length[:, None]).reshape(-1, 1)
    frame_mask = valid.astype(jnp.float32)
    projected = jnp.dot(normed, weights, preferred_element_type=jnp.float32) + biases.astype(
        jnp.float32
    )
    features = (projected * frame_mask).astype(jnp.bfloat16).reshape(slot_count, frame_count, -1)
    cot_rows = cotangent.reshape(slot_count * frame_count, -1)
    grad_out = jnp.where(valid, cot_rows, jnp.zeros_like(cot_rows))
    weight_term = lax.dot_general(
        normed, grad_out, (((0,), (0,)), ((), ())), preferred_element_type=jnp.float32
    )
    bias_term = jnp.sum(grad_out, axis=0, dtype=jnp.float32)
    part_weight, part_bias = (
        lax.psum_scatter(weight_term, "fsdp", scatter_dimension=1, tiled=True),
        lax.psum_scatter(bias_term, "fsdp", scatter_dimension=0, tiled=True),
    )
    grad_weight, grad_bias = lax.psum((part_weight, part_bias), "dp")
    return (features, grad_weight.astype(jnp.bfloat16), grad_bias.astype(jnp.bfloat16))


def solution(mesh):
    in_specs = (
        P(("dp", "fsdp"), None),
        P(("dp", "fsdp"), None),
        P(("dp", "fsdp")),
        P(),
        P(),
        P(),
        P(),
        P(None, "fsdp"),
        P("fsdp"),
        P(("dp", "fsdp"), None, None),
    )
    out_specs = (P(("dp", "fsdp"), None, None), P(None, "fsdp"), P("fsdp"))
    body = local_fused if (mesh.shape["dp"], mesh.shape["fsdp"]) == (8, 4) else local
    return jax.shard_map(body, mesh=mesh, in_specs=in_specs, out_specs=out_specs, check_vma=False)
```

```python
import functools
import math

import jax
import jax.numpy as jnp
from jax import lax
from jax.experimental import pallas as pl
from jax.experimental.pallas import tpu as pltpu
from jax.sharding import PartitionSpec as P

MESH = pl.DeviceIdType.MESH
F32 = jnp.float32
BF16 = jnp.bfloat16


def gelu(v):
    return 0.5 * v * (1.0 + lax.erf(v * (1.0 / math.sqrt(2.0))))


def norm_rows(values, gain_vec, bias_vec):
    avg = jnp.mean(values, axis=-1, keepdims=True)
    centred = values - avg
    var = jnp.mean(centred * centred, axis=-1, keepdims=True)
    return centred * lax.rsqrt(var + 1e-05) * gain_vec + bias_vec


def dot_t(a, b):
    return lax.dot_general(a, b, (((0,), (0,)), ((), ())), preferred_element_type=F32)


def fused(
    samp, n_dp, n_f, cap, frames,
    wave_ref, dest_ref, len_ref, w0_ref, w1_hbm, gain_ref, nbias_ref, pw_ref, pb_ref, cot_ref,
    feat_ref, gw_ref, gb_ref,
    w1_ref, w1_sem, perm_ref, table_ref, xsend, xrecv, w0p, wfull, pbfull, cotb, normed_ref, masked_ref, mask_ref,
    asend, arecv, gown, bsend, brecv, csend, crecv, gwbuf,
    hsend, hrecv, hsum, hall,
    x_s, x_r, wz_s, wz_r, wp_s, wp_r, wm_s, wm_r, pb_s, pb_r,
    a_s, a_r, b_s, b_r, c_s, c_r, d_s, d_r, e_s, e_r, h_s, h_r, k_s, k_r,
):
    d = lax.axis_index("dp")
    f = lax.axis_index("fsdp")
    core = d % 2
    chip = d // 2
    cx = chip % 2
    cy = chip // 2
    n_chip = n_dp // 2
    cols, depth = pw_ref.shape
    half = depth // 2
    ch = half // n_chip
    slots = n_dp * cap
    mate = chip * 2 + (1 - core)

    def other(c):
        return ((cy + c // 2) % 2) * 2 + (cx + c % 2) % 2

    def copy(src, dst, s_sem, r_sem, dd, ff):
        return pltpu.make_async_remote_copy(
            src_ref=src, dst_ref=dst, send_sem=s_sem, recv_sem=r_sem,
            device_id=(dd, ff), device_id_type=MESH,
        )

    w1_cp = pltpu.make_async_copy(w1_hbm, w1_ref, w1_sem)
    w1_cp.start()
    barrier = pltpu.get_barrier_semaphore()
    for o in range(1, n_dp):
        pl.semaphore_signal(barrier, inc=1, device_id=((d + o) % n_dp, f), device_id_type=MESH)
    for o in range(1, n_f):
        pl.semaphore_signal(barrier, inc=1, device_id=(d, (f + o) % n_f), device_id_type=MESH)

    rows = wave_ref.shape[0]
    tri_r = lax.broadcasted_iota(jnp.int32, (rows, rows), 0)
    tri_c = lax.broadcasted_iota(jnp.int32, (rows, rows), 1)
    lane = lax.broadcasted_iota(jnp.int32, (rows, 128), 1)
    spread = jnp.broadcast_to(len_ref[...].astype(F32), (rows, rows))
    span = jnp.sum(jnp.where(tri_r == tri_c, spread, 0.0), axis=1, keepdims=True)
    table_ref[...] = jnp.where(lane == samp, span, 0.0).astype(BF16)
    table_ref[:, 0:samp] = wave_ref[...]
    table = table_ref[...]
    lane = lane.astype(F32)
    named_row = jnp.broadcast_to(dest_ref[...].astype(F32), (rows, rows))
    target = jnp.sum(jnp.where(tri_r == tri_c, named_row, 0.0), axis=1, keepdims=True)
    named = (target == lane).astype(F32)
    earlier = (tri_c < tri_r).astype(F32).astype(BF16)
    before = jnp.dot(earlier, named.astype(BF16), preferred_element_type=F32)
    rank = jnp.sum(before * named, axis=1, keepdims=True)
    place = target * cap + rank
    placing = (place == lane).astype(F32).astype(BF16)
    placed = dot_t(placing, table)[:slots]
    xsend[...] = placed.reshape(n_dp, cap, 128)
    pl.semaphore_wait(barrier, n_dp + n_f - 2)

    x_cp = []
    for o in range(1, n_dp):
        p = (d + o) % n_dp
        x_cp.append(copy(xsend.at[p], xrecv.at[d], x_s.at[o], x_r.at[o], p, f))
        x_cp[-1].start()
    eye_r = lax.broadcasted_iota(jnp.int32, (depth, depth), 0)
    eye_c = lax.broadcasted_iota(jnp.int32, (depth, depth), 1)
    eye = (eye_r == eye_c).astype(F32).astype(BF16)
    wfull[f] = lax.dot_general(
        eye, pw_ref[...], (((1,), (1,)), ((), ())), preferred_element_type=F32).astype(BF16)
    pbfull[f] = jnp.broadcast_to(pb_ref[...].astype(F32)[None, :], (8, cols))
    mine = core * half + chip * ch
    z_cp, pb_cp = [], []
    for o in range(1, n_f):
        p = (f + o) % n_f
        z_cp.append(copy(
            wfull.at[f, pl.ds(mine, ch)], wfull.at[f, pl.ds(mine, ch)],
            wz_s.at[o], wz_r.at[o], d, p))
        z_cp[-1].start()
        pb_cp.append(copy(pbfull.at[f], pbfull.at[f], pb_s.at[o], pb_r.at[o], d, p))
        pb_cp[-1].start()
    xrecv[d] = xsend[d]
    w0p[...] = jnp.zeros_like(w0p)
    w0p[0 : w0_ref.shape[0], :] = w0_ref[...]
    total = slots * frames
    pr = lax.broadcasted_iota(jnp.int32, (total, total), 0)
    pc = lax.broadcasted_iota(jnp.int32, (total, total), 1) * frames
    hit = pr == pc
    for j in range(1, frames):
        hit = hit | (pr == pc - j * (total - 1))
    perm_ref[...] = hit.astype(F32).astype(BF16)
    for b in range(n_f):
        cotb[b] = cot_ref[:, b * cols : (b + 1) * cols]
    for o in range(1, n_dp):
        q = (d + n_dp - o) % n_dp
        copy(xsend.at[q], xrecv.at[q], x_s.at[o], x_r.at[o], q, f).wait_recv()

    x = xrecv[...].reshape(slots, 128)
    length = x[:, samp : samp + 1]
    first, p_cp = [], []
    for t in range(2 * frames + 1):
        xt = x if t == 0 else pltpu.roll(x, 128 - 5 * t, axis=1)
        v = jnp.dot(xt.astype(BF16), w0p[...], preferred_element_type=F32)
        first.append(gelu(norm_rows(v, gain_ref[0:1], nbias_ref[0:1])).astype(BF16))
        for o in range(1, n_f):
            if t != (2 * frames + 1) * o // n_f:
                continue
            q = (f + n_f - o) % n_f
            part = wfull.at[q, pl.ds(mine, ch)]
            copy(part, part, wz_s.at[o], wz_r.at[o], d, q).wait_recv()
            for c in range(1, n_chip):
                i = o * n_chip + c
                p_cp.append(copy(part, part, wp_s.at[i], wp_r.at[i], other(c) * 2 + core, f))
                p_cp[-1].start()

    w1_cp.wait()
    normed, masked, masks = [], [], []
    for j in range(frames):
        taps = jnp.concatenate(first[2 * j : 2 * j + 3], axis=1)
        v = jnp.dot(taps, w1_ref[...], preferred_element_type=F32)
        hid = gelu(norm_rows(v, gain_ref[1:2], nbias_ref[1:2])).astype(BF16).astype(F32)
        nj = norm_rows(hid, gain_ref[2:3], nbias_ref[2:3]).astype(BF16)
        mj = (length >= 10.0 * j + 20.0).astype(F32)
        normed.append(nj)
        masks.append(jnp.broadcast_to(mj, (slots, 128)).astype(BF16))
    nrm = jnp.dot(perm_ref[...], jnp.concatenate(normed, axis=0), preferred_element_type=F32)
    msk = jnp.dot(perm_ref[...], jnp.concatenate(masks, axis=0), preferred_element_type=F32)
    normed_ref[...] = nrm.astype(BF16)
    masked_ref[...] = (nrm * msk[:, 0:1]).astype(BF16)
    mask_ref[...] = msk

    order = [o % n_f for o in range(1, n_f + 1)]
    a_cp = []
    theirs = masked_ref[:, pl.ds(pl.multiple_of((1 - core) * half, half), half)]
    for o in order:
        b = (f + o) % n_f
        asend[o] = dot_t(theirs, cotb[b]).astype(BF16)
        a_cp.append(copy(asend.at[o], arecv.at[o], a_s.at[o], a_r.at[o], mate, f))
        a_cp[-1].start()
    ours = masked_ref[:, pl.ds(pl.multiple_of(core * half, half), half)]
    for o in order:
        b = (f + o) % n_f
        gown[o] = dot_t(ours, cotb[b])
    b_cp = []
    for o in order:
        copy(asend.at[o], arecv.at[o], a_s.at[o], a_r.at[o], mate, f).wait_recv()
        both = gown[o] + arecv[o].astype(F32)
        gown[o] = both
        bsend[o] = both.astype(BF16)
        for c in range(1, n_chip):
            to = other(c)
            i = o * n_chip + c
            b_cp.append(copy(
                bsend.at[o, pl.ds(to * ch, ch)], brecv.at[i],
                b_s.at[i], b_r.at[i], to * 2 + core, f))
            b_cp[-1].start()

    h_cp = []
    ones = mask_ref[...].astype(BF16)
    for o in order:
        b = (f + o) % n_f
        hsend[o] = dot_t(ones, cotb[b])[0:8]
        if o:
            h_cp.append(copy(hsend.at[o], hrecv.at[o], h_s.at[o], h_r.at[o], d, b))
            h_cp[-1].start()

    c_cp = []
    own = None
    for o in order:
        part = gown[o, pl.ds(chip * ch, ch), :]
        for c in range(1, n_chip):
            i = o * n_chip + c
            copy(brecv.at[i], brecv.at[i], b_s.at[i], b_r.at[i], other(c) * 2 + core, f).wait_recv()
            part = part + brecv[i].astype(F32)
        if o:
            csend[o] = part.astype(BF16)
            c_cp.append(copy(csend.at[o], crecv.at[o], c_s.at[o], c_r.at[o], d, (f + o) % n_f))
            c_cp[-1].start()
        else:
            own = part
    m_cp = []
    for o in range(1, n_f):
        q = (f + n_f - o) % n_f
        for c in range(1, n_chip):
            i = o * n_chip + c
            theirs_at = core * half + other(c) * ch
            part = wfull.at[q, pl.ds(theirs_at, ch)]
            copy(part, part, wp_s.at[i], wp_r.at[i], other(c) * 2 + core, f).wait_recv()
        block = wfull.at[q, pl.ds(core * half, half)]
        m_cp.append(copy(block, block, wm_s.at[o], wm_r.at[o], mate, f))
        m_cp[-1].start()
        copy(pbfull.at[q], pbfull.at[q], pb_s.at[o], pb_r.at[o], d, q).wait_recv()
    hown = hsend[0]
    for o in range(1, n_f):
        q = (f + n_f - o) % n_f
        copy(hsend.at[o], hrecv.at[o], h_s.at[o], h_r.at[o], d, q).wait_recv()
        hown = hown + hrecv[o]
    hsum[...] = hown
    k_cp = []
    for o in range(1, n_dp):
        k_cp.append(copy(hsum, hall.at[o], k_s.at[o], k_r.at[o], (d + o) % n_dp, f))
        k_cp[-1].start()
    for o in range(1, n_f):
        q = (f + n_f - o) % n_f
        copy(csend.at[o], crecv.at[o], c_s.at[o], c_r.at[o], d, q).wait_recv()
        own = own + crecv[o].astype(F32)
    gwbuf[pl.ds(mine, ch), :] = own.astype(BF16)

    d_cp = []
    src = gwbuf.at[pl.ds(mine, ch)]
    for c in range(1, n_chip):
        d_cp.append(copy(src, src, d_s.at[c], d_r.at[c], other(c) * 2 + core, f))
        d_cp[-1].start()
    e_cp = [copy(src, src, e_s.at[0], e_r.at[0], mate, f)]
    e_cp[0].start()
    for o in range(1, n_f):
        q = (f + n_f - o) % n_f
        block = wfull.at[q, pl.ds((1 - core) * half, half)]
        copy(block, block, wm_s.at[o], wm_r.at[o], mate, f).wait_recv()
    def project(b):
        v = jnp.dot(normed_ref[...], wfull[b], preferred_element_type=F32) + pbfull[b][0:1]
        feat_ref[:, b * cols : (b + 1) * cols] = (v * mask_ref[:, 0:1]).astype(BF16)

    for b in range(n_f):
        project(b)

    for c in range(1, n_chip):
        part = gwbuf.at[pl.ds(core * half + other(c) * ch, ch)]
        copy(part, part, d_s.at[c], d_r.at[c], other(c) * 2 + core, f).wait_recv()
        e_cp.append(copy(part, part, e_s.at[c], e_r.at[c], mate, f))
        e_cp[-1].start()
    for o in range(1, n_dp):
        copy(hsum, hall.at[o], k_s.at[o], k_r.at[o], (d + n_dp - o) % n_dp, f).wait_recv()
        hown = hown + hall[o]
    gb_ref[...] = hown[0].astype(BF16)
    for c in range(n_chip):
        at = other(c) if c else chip
        part = gwbuf.at[pl.ds((1 - core) * half + at * ch, ch)]
        copy(part, part, e_s.at[c], e_r.at[c], mate, f).wait_recv()
    gw_ref[...] = dot_t(gwbuf[...], eye).astype(BF16)
    for one in x_cp + z_cp + pb_cp + p_cp + m_cp + a_cp + h_cp + b_cp + c_cp + k_cp + d_cp + e_cp:
        one.wait_send()


def local_fused(
    waveform, destination, lengths, conv0_weight, conv1_weight,
    norm_gain, norm_bias, proj_weight, proj_bias, cotangent,
):
    n_dp, n_f = lax.axis_size("dp"), lax.axis_size("fsdp")
    rows, samp = waveform.shape
    slots, frames, width = cotangent.shape
    cap = slots // n_dp
    depth, cols = proj_weight.shape
    n_chip, half = n_dp // 2, depth // 2
    ch = half // n_chip
    total = slots * frames
    vmem = pl.BlockSpec(memory_space=pltpu.VMEM)
    hbm = pl.BlockSpec(memory_space=pltpu.HBM)
    dma = lambda n: pltpu.SemaphoreType.DMA((n,))
    nc = n_f * n_chip
    feats, gw, gb = pl.pallas_call(
        functools.partial(fused, samp, n_dp, n_f, cap, frames),
        out_shape=(
            jax.ShapeDtypeStruct((total, width), BF16),
            jax.ShapeDtypeStruct((cols, depth), BF16),
            jax.ShapeDtypeStruct((cols,), BF16),
        ),
        in_specs=[vmem] * 4 + [hbm] + [vmem] * 5,
        out_specs=(vmem,) * 3,
        scratch_shapes=[
            pltpu.VMEM(conv1_weight.shape, BF16),
            pltpu.SemaphoreType.DMA,
            pltpu.VMEM((total, total), BF16),
            pltpu.VMEM((rows, 128), BF16),
            pltpu.VMEM((n_dp, cap, 128), F32),
            pltpu.VMEM((n_dp, cap, 128), F32),
            pltpu.VMEM((128, depth), BF16),
            pltpu.VMEM((n_f, depth, cols), BF16),
            pltpu.VMEM((n_f, 8, cols), F32),
            pltpu.VMEM((n_f, total, cols), BF16),
            pltpu.VMEM((total, depth), BF16),
            pltpu.VMEM((total, depth), BF16),
            pltpu.VMEM((total, 128), F32),
            pltpu.VMEM((n_f, half, cols), BF16),
            pltpu.VMEM((n_f, half, cols), BF16),
            pltpu.VMEM((n_f, half, cols), F32),
            pltpu.VMEM((n_f, half, cols), BF16),
            pltpu.VMEM((nc, ch, cols), BF16),
            pltpu.VMEM((n_f, ch, cols), BF16),
            pltpu.VMEM((n_f, ch, cols), BF16),
            pltpu.VMEM((depth, cols), BF16),
            pltpu.VMEM((n_f, 8, cols), F32),
            pltpu.VMEM((n_f, 8, cols), F32),
            pltpu.VMEM((8, cols), F32),
            pltpu.VMEM((n_dp, 8, cols), F32),
            dma(n_dp), dma(n_dp), dma(n_f), dma(n_f), dma(nc), dma(nc),
            dma(n_f), dma(n_f), dma(n_f), dma(n_f),
            dma(n_f), dma(n_f), dma(nc), dma(nc), dma(n_f), dma(n_f),
            dma(n_chip), dma(n_chip), dma(n_chip), dma(n_chip),
            dma(n_f), dma(n_f), dma(n_dp), dma(n_dp),
        ],
        compiler_params=pltpu.CompilerParams(
            collective_id=0, has_side_effects=True, vmem_limit_bytes=48 * 1024 * 1024),
        cost_estimate=pl.CostEstimate(
            flops=2 * total * depth * (3 * depth + 2 * width),
            bytes_accessed=8 * depth * width, transcendentals=13 * slots * depth),
    )(waveform, destination.reshape(1, -1), lengths[None, :], conv0_weight, conv1_weight,
      norm_gain, norm_bias, proj_weight.T, proj_bias, cotangent.reshape(total, width))
    return feats.reshape(slots, frames, width), gw.T, gb


def layer_norm(values, gain_vec, bias_vec):
    avg_value = jnp.mean(values, axis=-1, keepdims=True)
    centred = values - avg_value
    variance = jnp.mean(centred * centred, axis=-1, keepdims=True)
    return centred * lax.rsqrt(variance + 1e-05) * gain_vec + bias_vec


def encode(wave_rows, conv0_weight, conv1_weight, norm_gain, norm_bias):
    row_count = wave_rows.shape[0]
    frame_count = (wave_rows.shape[1] - 10) // 10
    sample_blocks = wave_rows.reshape(row_count, 2 * frame_count + 2, 5)
    sample_pairs = jnp.concatenate([sample_blocks[:, :-1], sample_blocks[:, 1:]], axis=2).reshape(
        -1, 10
    )
    first_conv = jnp.dot(sample_pairs, conv0_weight, preferred_element_type=jnp.float32)
    first_conv = jax.nn.gelu(
        layer_norm(first_conv, norm_gain[0], norm_bias[0]), approximate=False
    ).astype(jnp.bfloat16)
    first_conv = first_conv.reshape(row_count, 2 * frame_count + 1, -1)
    conv_taps = jnp.concatenate(
        [
            first_conv[:, 0 : 2 * frame_count : 2],
            first_conv[:, 1 : 2 * frame_count + 1 : 2],
            first_conv[:, 2 : 2 * frame_count + 2 : 2],
        ],
        axis=2,
    )
    second_conv = jnp.dot(
        conv_taps.reshape(row_count * frame_count, -1),
        conv1_weight,
        preferred_element_type=jnp.float32,
    )
    return jax.nn.gelu(
        layer_norm(second_conv, norm_gain[1], norm_bias[1]), approximate=False
    ).astype(jnp.bfloat16)


def local(
    waveform,
    destination,
    lengths,
    conv0_weight,
    conv1_weight,
    norm_gain,
    norm_bias,
    proj_weight,
    proj_bias,
    cotangent,
):
    dp_size = lax.axis_size("dp")
    row_count = waveform.shape[0]
    slot_count = cotangent.shape[0]
    frame_count = cotangent.shape[1]
    slot_cap = slot_count // dp_size
    weights, biases = (
        lax.all_gather(proj_weight, "fsdp", axis=1, tiled=True),
        lax.all_gather(proj_bias, "fsdp", axis=0, tiled=True),
    )
    targets = destination[:, 0]
    row_order = jnp.arange(row_count, dtype=jnp.int32)
    same_dest = targets[:, None] == targets[None, :]
    earlier_rows = row_order[None, :] < row_order[:, None]
    row_rank = jnp.sum((same_dest & earlier_rows).astype(jnp.int32), axis=1)
    position = targets * slot_cap + row_rank
    placing = position[None, :] == jnp.arange(slot_count, dtype=jnp.int32)[:, None]
    slot_length = jnp.sum(jnp.where(placing, lengths[None, :], 0), axis=1)
    placing_matrix = placing.astype(jnp.bfloat16)
    slot_wave = jnp.dot(placing_matrix, waveform, preferred_element_type=jnp.float32).astype(
        jnp.bfloat16
    )
    got_wave, got_length = (
        lax.all_to_all(
            slot_wave.reshape(dp_size, slot_cap, -1), "dp", split_axis=0, concat_axis=0, tiled=True
        ),
        lax.all_to_all(
            slot_length.reshape(dp_size, slot_cap), "dp", split_axis=0, concat_axis=0, tiled=True
        ),
    )
    hidden = encode(
        got_wave.reshape(slot_count, -1), conv0_weight, conv1_weight, norm_gain, norm_bias
    )
    got_length = got_length.reshape(slot_count)
    normed = layer_norm(hidden.astype(jnp.float32), norm_gain[2], norm_bias[2]).astype(jnp.bfloat16)
    frame_ids = jnp.arange(frame_count, dtype=jnp.int32)
    valid = (10 * frame_ids[None, :] + 20 <= got_length[:, None]).reshape(-1, 1)
    frame_mask = valid.astype(jnp.float32)
    projected = jnp.dot(normed, weights, preferred_element_type=jnp.float32) + biases.astype(
        jnp.float32
    )
    features = (projected * frame_mask).astype(jnp.bfloat16).reshape(slot_count, frame_count, -1)
    cot_rows = cotangent.reshape(slot_count * frame_count, -1)
    grad_out = jnp.where(valid, cot_rows, jnp.zeros_like(cot_rows))
    weight_term = lax.dot_general(
        normed, grad_out, (((0,), (0,)), ((), ())), preferred_element_type=jnp.float32
    )
    bias_term = jnp.sum(grad_out, axis=0, dtype=jnp.float32)
    part_weight, part_bias = (
        lax.psum_scatter(weight_term, "fsdp", scatter_dimension=1, tiled=True),
        lax.psum_scatter(bias_term, "fsdp", scatter_dimension=0, tiled=True),
    )
    grad_weight, grad_bias = lax.psum((part_weight, part_bias), "dp")
    return (features, grad_weight.astype(jnp.bfloat16), grad_bias.astype(jnp.bfloat16))


def solution(mesh):
    in_specs = (
        P(("dp", "fsdp"), None),
        P(("dp", "fsdp"), None),
        P(("dp", "fsdp")),
        P(),
        P(),
        P(),
        P(),
        P(None, "fsdp"),
        P("fsdp"),
        P(("dp", "fsdp"), None, None),
    )
    out_specs = (P(("dp", "fsdp"), None, None), P(None, "fsdp"), P("fsdp"))
    body = local_fused if (mesh.shape["dp"], mesh.shape["fsdp"]) == (8, 4) else local
    return jax.shard_map(body, mesh=mesh, in_specs=in_specs, out_specs=out_specs, check_vma=False)
```
